128 devices in a mesh: rows: 32 (over z, y, core), cols: 4 (over x).
Axes of the slice: x: 4, y: 4, z: 4, core: 2. Of those that a mesh axis runs over, the one named last changes fastest.
Arguments:
- snapshots: float32 [65536, 4096], P('rows', 'cols'), may hold values from -27 to 27
Outputs:
- r_factor: float32 [128, 128], replicated
- coupling: float32 [128, 4096], P(None, 'cols')
- updated: float32 [65536, 4096], P('rows', 'cols')
The draws below stay inside these ranges and needn't reach their ends.
All inputs are finite; a program needn't handle non-finite values.
Results may differ from the reference program's by a relative error of at most 0.00025.
Values sent between devices are 32-bit elements; how exact they have to be, the bound alone decides.
A program may use at most 64 MiB of HBM per device.

```python
import math
import jax
import jax.numpy as jnp
from jax import lax

PANEL = 128
TOTAL_ROWS = 65536
TOTAL_SNAPS = 4096


def draw_snapshots(key, part):
    key = jax.random.fold_in(key, 7)
    keys = jax.random.split(key, 3)
    shape = (TOTAL_ROWS, TOTAL_SNAPS)
    base = jax.random.truncated_normal(keys[0], -4.0, 4.0, shape, jnp.float32)
    position = jnp.arange(TOTAL_ROWS, dtype=jnp.float32)[:, None] / TOTAL_ROWS
    row_scale = jnp.exp(position * jnp.log(3.0)) * jnp.exp(jax.random.uniform(keys[1], (TOTAL_ROWS, 1), jnp.float32, -0.69, 0.4))
    col_scale = jnp.exp(jax.random.uniform(keys[2], (1, TOTAL_SNAPS), jnp.float32, -0.69, 0.4))
    return base * row_scale * col_scale


def setup_inputs(seed: int = 0) -> dict:
    arg_keys = jax.random.split(jax.random.key(seed), 2)
    return {
        "snapshots": draw_snapshots(jax.random.fold_in(arg_keys[1], 71), 0),
    }


def factor(gram):
    width = gram.shape[0]
    columns = jnp.arange(width, dtype=jnp.int32)

    def advance(position, carry):
        remaining, upper = carry
        current = lax.dynamic_index_in_dim(remaining, position, 0, keepdims=False)
        pivot_value = lax.dynamic_index_in_dim(current, position, 0, keepdims=False)
        current = jnp.where(columns >= position, current / jnp.sqrt(pivot_value), jnp.zeros_like(current))
        remaining = remaining - current[:, None] * current[None, :]
        upper = lax.dynamic_update_index_in_dim(upper, current, position, 0)
        return (remaining, upper)
    return lax.fori_loop(0, width, advance, (gram, jnp.zeros_like(gram)))[1]

def invert_upper(upper):
    width = upper.shape[0]
    columns = jnp.arange(width, dtype=jnp.int32)
    identity = jnp.eye(width, dtype=upper.dtype)

    def advance(backward, inverse):
        position = width - 1 - backward
        current = lax.dynamic_index_in_dim(upper, position, 0, keepdims=False)
        diagonal_entry = lax.dynamic_index_in_dim(current, position, 0, keepdims=False)
        beyond = jnp.where(columns > position, current, jnp.zeros_like(current))
        target = lax.dynamic_index_in_dim(identity, position, 0, keepdims=False)
        fresh = (target - jnp.dot(beyond, inverse, precision=lax.Precision.HIGHEST)) / diagonal_entry
        return lax.dynamic_update_index_in_dim(inverse, fresh, position, 0)
    return lax.fori_loop(0, width, advance, jnp.zeros_like(upper))

def reference(snapshots):
    highest = lax.Precision.HIGHEST
    panel = snapshots[:, :PANEL]
    gram = jnp.dot(panel.T, panel, precision=highest, preferred_element_type=jnp.float32)
    upper = factor(gram)
    basis = jnp.dot(panel, invert_upper(upper), precision=highest, preferred_element_type=jnp.float32)
    coupling = jnp.dot(basis.T, snapshots, precision=highest, preferred_element_type=jnp.float32)
    updated = snapshots - jnp.dot(basis, coupling, precision=highest, preferred_element_type=jnp.float32)
    return (upper / math.sqrt(TOTAL_ROWS), coupling, updated)
```

```python
import jax
import jax.numpy as jnp
from jax import lax
from jax.experimental import pallas as pl
from jax.experimental.pallas import tpu as pltpu
from jax.sharding import PartitionSpec as P

MESH = pl.DeviceIdType.MESH
F32 = jnp.float32
BF16 = jnp.bfloat16
PANEL = 128
ROWS = 2048
COLS = 1024
HALF = COLS // 2
CHIPS = 16
BLOCK = 256
BLOCKS = ROWS // BLOCK
CHUNK = 64
CHUNKS = ROWS // CHUNK
SIDE = CHUNKS // 2
PER = BLOCK // CHUNK
PIECE = PANEL // CHIPS
GROUP = 16


def split(value):
    high = value.astype(BF16)
    low = (value - high.astype(F32)).astype(BF16)
    return high, low


def cross(left, right):
    return lax.dot_general(left, right, (((0,), (0,)), ((), ())), preferred_element_type=F32)


def plain(left, right):
    return lax.dot_general(left, right, (((1,), (0,)), ((), ())), preferred_element_type=F32)


def cholesky(gram, packed_ref):
    sub = lax.broadcasted_iota(jnp.int32, (GROUP, PANEL), 0)
    lane = lax.broadcasted_iota(jnp.int32, (GROUP, PANEL), 1)
    eye = (
        lax.broadcasted_iota(jnp.int32, (PANEL, PANEL), 0)
        == lax.broadcasted_iota(jnp.int32, (PANEL, PANEL), 1)
    ).astype(F32)

    def step(block, carry):
        left, right = carry
        top, side = left[:GROUP], right[:GROUP]
        pivots = jnp.ones((GROUP, PANEL), F32)
        for k in range(GROUP):
            column = jnp.broadcast_to(top[:, k : k + 1], (GROUP, PANEL))
            pivot = jnp.broadcast_to(column[k : k + 1, :], (GROUP, PANEL))
            factor = jnp.where(sub > k, column * (1.0 / pivot), 0.0)
            pivots = jnp.where(sub == k, pivot, pivots)
            if k < GROUP - 1:
                row = jnp.broadcast_to(top[k : k + 1, :], (GROUP, PANEL))
                other = jnp.broadcast_to(side[k : k + 1, :], (GROUP, PANEL))
                top = top - factor * row
                side = side - factor * other
        scale = lax.rsqrt(pivots)
        scale = scale * (1.5 - 0.5 * pivots * scale * scale)
        top = jnp.where(lane >= sub, top * scale, 0.0)
        side = side * scale
        update = lax.dot_general(
            top,
            jnp.concatenate([top, side], axis=1),
            (((0,), (0,)), ((), ())),
            precision=lax.Precision.HIGHEST,
            preferred_element_type=F32,
        )
        left = left - update[:, :PANEL]
        right = right - update[:, PANEL:]
        base = pl.multiple_of(block * GROUP, GROUP)
        upper = pltpu.roll(top, base, 1)
        packed_ref[pl.ds(base, GROUP), :] = jnp.where(lane >= sub + base, upper, side)
        left = jnp.concatenate([left[GROUP:], left[:GROUP]], axis=0)
        left = pltpu.roll(left, PANEL - GROUP, 1)
        right = jnp.concatenate([right[GROUP:], right[:GROUP]], axis=0)
        return left, right

    lax.fori_loop(0, PANEL // GROUP, step, (gram, eye))


def gather_kernel(
    snap, kept, panel2, total, packed,
    pbuf, high, low, wacc, swap, mine, parts, gram, gparts, gsum, gswap, gfull,
    load_sem, pload_sem, bs_send, bs_recv, ex_send, ex_recv, rs_send, rs_recv, ag_send, ag_recv,
    fx_send, fx_recv, gr_send, gr_recv, gx_send, gx_recv, ga_send, ga_recv, u_send, u_recv,
):
    row = lax.axis_index("rows")
    col = lax.axis_index("cols")
    chip = row // 2
    core = row % 2
    partner = (chip * 2 + 1 - core, col)

    def peer(step):
        return ((chip + step) % CHIPS) * 2 + core

    barrier = pltpu.get_barrier_semaphore()
    for step in (1, 2, 3):
        pl.semaphore_signal(barrier, inc=1, device_id=(row, (col + step) % 4), device_id_type=MESH)
    pl.semaphore_signal(barrier, inc=1, device_id=partner, device_id_type=MESH)

    def greet(step, carry):
        pl.semaphore_signal(barrier, inc=1, device_id=(peer(step), col), device_id_type=MESH)
        return carry

    lax.fori_loop(1, CHIPS, greet, 0)

    def load(block):
        rows = pl.ds(pl.multiple_of(block * BLOCK, BLOCK), BLOCK)
        return pltpu.make_async_copy(snap.at[rows], kept.at[rows], load_sem.at[block])

    panel_load = pltpu.make_async_copy(snap.at[:, pl.ds(0, PANEL)], pbuf, pload_sem)

    @pl.when(col == 0)
    def _():
        panel_load.start()

    def start_load(block, carry):
        load(block).start()
        return carry

    lax.fori_loop(0, BLOCKS, start_load, 0)
    pl.semaphore_wait(barrier, CHIPS + 3)

    def chunk_rows(chunk):
        return pl.ds(pl.multiple_of(chunk * CHUNK, CHUNK), CHUNK)

    def relay(chunk, target):
        rows = chunk_rows(chunk)
        return pltpu.make_async_remote_copy(
            src_ref=pbuf.at[rows], dst_ref=pbuf.at[rows], send_sem=bs_send.at[chunk],
            recv_sem=bs_recv.at[chunk], device_id=(row, target), device_id_type=MESH,
        )

    def first(chunk, target):
        rows = chunk_rows(chunk)
        return pltpu.make_async_remote_copy(
            src_ref=snap.at[rows, pl.ds(0, PANEL)], dst_ref=pbuf.at[rows], send_sem=bs_send.at[chunk],
            recv_sem=bs_recv.at[chunk], device_id=(row, target), device_id_type=MESH,
        )

    @pl.when(col == 0)
    def _():
        def send(step, carry):
            first(step, 1).start()
            first(step + SIDE, 3).start()
            return carry

        lax.fori_loop(0, SIDE, send, 0)

    def block_rows(block):
        return pl.ds(pl.multiple_of(block * BLOCK, BLOCK), BLOCK)

    def widen(block):
        rows = block_rows(block)
        ph, plo = split(pbuf[rows])
        panel2[rows, :PANEL] = ph
        panel2[rows, PANEL:] = plo

    def prepare(block, carry):
        load(block).wait()
        rows = block_rows(block)
        sh, sl = split(kept[rows])
        high[rows] = sh
        low[rows] = sl
        return carry

    def accumulate(block):
        rows = block_rows(block)
        both = panel2[rows]
        for n in range(COLS // 256):
            columns = pl.ds(n * 256, 256)
            one = cross(both, high[rows, columns])
            two = cross(both[:, :PANEL], low[rows, columns])
            wacc[:, columns] += one[:PANEL] + one[PANEL:] + two

    def gram_piece(step):
        other = (chip + step) % CHIPS
        return pltpu.make_async_remote_copy(
            src_ref=gram.at[pl.ds(pl.multiple_of(other * PIECE, PIECE), PIECE)], dst_ref=gparts.at[chip],
            send_sem=gr_send.at[step], recv_sem=gr_recv.at[chip], device_id=(peer(step), col), device_id_type=MESH,
        )

    def gram_arrived(step):
        other = (chip + step) % CHIPS
        return pltpu.make_async_remote_copy(
            src_ref=gram.at[pl.ds(0, PIECE)], dst_ref=gparts.at[other],
            send_sem=gr_send.at[step], recv_sem=gr_recv.at[other], device_id=(peer(step), col), device_id_type=MESH,
        )

    @pl.when(col == 0)
    def _():
        panel_load.wait()

        def one(block, carry):
            widen(block)
            return carry

        lax.fori_loop(0, BLOCKS, one, 0)
        full = cross(panel2[...], panel2[...])
        gram[...] = full[:PANEL, :PANEL] + (full[:PANEL, PANEL:] + full[PANEL:, :PANEL]) + full[PANEL:, PANEL:]

        def send(step, carry):
            gram_piece(step).start()
            return carry

        lax.fori_loop(1, CHIPS, send, 0)
        gparts[chip] = gram[pl.ds(pl.multiple_of(chip * PIECE, PIECE), PIECE)]

    wacc[...] = jnp.zeros_like(wacc)
    lax.fori_loop(0, BLOCKS, prepare, 0)

    @pl.when(col == 0)
    def _():
        def one(block, carry):
            accumulate(block)
            return carry

        lax.fori_loop(0, BLOCKS, one, 0)

    @pl.when(col != 0)
    def _():
        def chunk_of(step):
            straight = (step + jnp.where(col == 3, SIDE, 0)) % CHUNKS
            return jnp.where(col == 2, (step % 2) * SIDE + step // 2, straight)

        def one(step, carry):
            chunk = chunk_of(step)
            onward = jnp.where(chunk < SIDE, col + 1, col - 1)
            relay(chunk, 0).wait_recv()

            @pl.when((onward > 0) & (onward < 4))
            def _():
                relay(chunk, onward).start()

            return carry

        def both(pair, carry):
            block_a = jnp.where(col == 2, pair, (2 * pair + jnp.where(col == 3, BLOCKS // 2, 0)) % BLOCKS)
            block_b = jnp.where(col == 2, pair + BLOCKS // 2, block_a + 1)
            start = pair * 2 * PER
            lax.fori_loop(start, start + PER, one, 0)

            @pl.when(col != 2)
            def _():
                widen(block_a)
                accumulate(block_a)

            lax.fori_loop(start + PER, start + 2 * PER, one, 0)

            @pl.when(col == 2)
            def _():
                widen(block_a)
                accumulate(block_a)

            widen(block_b)
            accumulate(block_b)
            return carry

        lax.fori_loop(0, BLOCKS // 2, both, 0)

    exchange = pltpu.make_async_remote_copy(
        src_ref=wacc.at[:, pl.ds(pl.multiple_of((1 - core) * HALF, HALF), HALF)], dst_ref=swap,
        send_sem=ex_send, recv_sem=ex_recv, device_id=partner, device_id_type=MESH,
    )
    exchange.start()

    gram_swap = pltpu.make_async_remote_copy(
        src_ref=gsum, dst_ref=gswap, send_sem=gx_send, recv_sem=gx_recv, device_id=partner, device_id_type=MESH,
    )

    def gram_gather(step):
        rows = pl.ds(pl.multiple_of(chip * PIECE, PIECE), PIECE)
        return pltpu.make_async_remote_copy(
            src_ref=gfull.at[rows], dst_ref=gfull.at[rows],
            send_sem=ga_send.at[step], recv_sem=ga_recv.at[chip], device_id=(peer(step), col), device_id_type=MESH,
        )

    def gram_gathered(step):
        other = (chip + step) % CHIPS
        rows = pl.ds(pl.multiple_of(other * PIECE, PIECE), PIECE)
        return pltpu.make_async_remote_copy(
            src_ref=gfull.at[rows], dst_ref=gfull.at[rows],
            send_sem=ga_send.at[step], recv_sem=ga_recv.at[other], device_id=(peer(step), col), device_id_type=MESH,
        )

    @pl.when(col == 0)
    def _():
        def wait(step, carry):
            gram_arrived(step).wait_recv()
            return carry

        lax.fori_loop(1, CHIPS, wait, 0)
        gsum[...] = jnp.sum(gparts[...], axis=0)
        gram_swap.start()
        gram_swap.wait()
        gfull[pl.ds(pl.multiple_of(chip * PIECE, PIECE), PIECE)] = gsum[...] + gswap[...]

        def send(step, carry):
            gram_gather(step).start()
            return carry

        lax.fori_loop(1, CHIPS, send, 0)

    exchange.wait()
    mine[...] = wacc[:, pl.ds(pl.multiple_of(core * HALF, HALF), HALF)] + swap[...]

    def scatter(step):
        other = (chip + step) % CHIPS
        return pltpu.make_async_remote_copy(
            src_ref=mine.at[pl.ds(pl.multiple_of(other * PIECE, PIECE), PIECE)], dst_ref=parts.at[chip],
            send_sem=rs_send.at[step], recv_sem=rs_recv.at[chip], device_id=(peer(step), col), device_id_type=MESH,
        )

    def scattered(step):
        other = (chip + step) % CHIPS
        return pltpu.make_async_remote_copy(
            src_ref=mine.at[pl.ds(0, PIECE)], dst_ref=parts.at[other],
            send_sem=rs_send.at[step], recv_sem=rs_recv.at[other], device_id=(peer(step), col), device_id_type=MESH,
        )

    def send_scatter(step, carry):
        scatter(step).start()
        return carry

    lax.fori_loop(1, CHIPS, send_scatter, 0)
    parts[chip] = mine[pl.ds(pl.multiple_of(chip * PIECE, PIECE), PIECE)]

    def send_packed(target):
        return pltpu.make_async_remote_copy(
            src_ref=packed, dst_ref=packed, send_sem=u_send.at[target], recv_sem=u_recv,
            device_id=(row, target), device_id_type=MESH,
        )

    @pl.when(col == 0)
    def _():
        def wait(step, carry):
            gram_gathered(step).wait_recv()
            return carry

        lax.fori_loop(1, CHIPS, wait, 0)
        cholesky(gfull[...], packed)
        for target in (2, 1, 3):
            send_packed(target).start()

    def wait_scatter(step, carry):
        scattered(step).wait_recv()
        return carry

    lax.fori_loop(1, CHIPS, wait_scatter, 0)
    half = pl.ds(pl.multiple_of(core * HALF, HALF), HALF)
    own = pl.ds(pl.multiple_of(chip * PIECE, PIECE), PIECE)
    total[own, half] = jnp.sum(parts[...], axis=0)

    def gather(step):
        return pltpu.make_async_remote_copy(
            src_ref=total.at[own, half], dst_ref=total.at[own, half],
            send_sem=ag_send.at[step], recv_sem=ag_recv.at[chip], device_id=(peer(step), col), device_id_type=MESH,
        )

    def gathered(step):
        other = (chip + step) % CHIPS
        rows = pl.ds(pl.multiple_of(other * PIECE, PIECE), PIECE)
        return pltpu.make_async_remote_copy(
            src_ref=total.at[rows, half], dst_ref=total.at[rows, half],
            send_sem=ag_send.at[step], recv_sem=ag_recv.at[other], device_id=(peer(step), col), device_id_type=MESH,
        )

    def send_gather(step, carry):
        gather(step).start()
        return carry

    lax.fori_loop(1, CHIPS, send_gather, 0)

    def wait_gather(step, carry):
        gathered(step).wait_recv()
        return carry

    lax.fori_loop(1, CHIPS, wait_gather, 0)
    other_half = pl.ds(pl.multiple_of((1 - core) * HALF, HALF), HALF)
    final = pltpu.make_async_remote_copy(
        src_ref=total.at[:, half], dst_ref=total.at[:, half], send_sem=fx_send, recv_sem=fx_recv,
        device_id=partner, device_id_type=MESH,
    )
    final.start()
    arrival = pltpu.make_async_remote_copy(
        src_ref=total.at[:, other_half], dst_ref=total.at[:, other_half], send_sem=fx_send, recv_sem=fx_recv,
        device_id=partner, device_id_type=MESH,
    )

    def finish(step, carry):
        scatter(step).wait_send()
        gather(step).wait_send()
        return carry

    lax.fori_loop(1, CHIPS, finish, 0)

    @pl.when(col == 0)
    def _():
        def end(step, carry):
            gram_piece(step).wait_send()
            gram_gather(step).wait_send()
            return carry

        lax.fori_loop(1, CHIPS, end, 0)
        for target in (2, 1, 3):
            send_packed(target).wait_send()

        def sent(chunk, carry):
            first(chunk, 1).wait_send()
            return carry

        lax.fori_loop(0, CHUNKS, sent, 0)

    @pl.when((col == 1) | (col == 2))
    def _():
        def sent(chunk, carry):
            relay(chunk, 0).wait_send()
            return carry

        lax.fori_loop(0, SIDE, sent, 0)

    @pl.when((col == 3) | (col == 2))
    def _():
        def sent(chunk, carry):
            relay(chunk, 0).wait_send()
            return carry

        lax.fori_loop(SIDE, CHUNKS, sent, 0)

    @pl.when(col != 0)
    def _():
        send_packed(0).wait_recv()

    final.wait_send()
    arrival.wait_recv()


def apply_kernel(kept, panel2, total, packed, factor, coupling, updated, out, x2, sems):
    both = packed[...]
    sub = lax.broadcasted_iota(jnp.int32, (PANEL, PANEL), 0)
    lane = lax.broadcasted_iota(jnp.int32, (PANEL, PANEL), 1)
    upper = jnp.where(lane >= sub, both, 0.0)
    factor[...] = upper * (1.0 / 256.0)
    lower = jnp.where(lane < sub, both, jnp.where(lane == sub, 1.0 / both, 0.0))
    lh, ll = split(lower)
    for n in range(COLS // 256):
        columns = pl.ds(n * 256, 256)
        wh, wl = split(total[:, columns])
        c = plain(lh, wh) + (plain(lh, wl) + plain(ll, wh))
        coupling[:, columns] = c
        ch, cl = split(c)
        x = cross(lh, ch) + (cross(lh, cl) + cross(ll, ch))
        xh, xl = split(x)
        x2[0:PANEL, columns] = xh
        x2[PANEL : 2 * PANEL, columns] = xh
        x2[2 * PANEL :, columns] = xl

    def write(block):
        rows = pl.ds(pl.multiple_of(block * BLOCK, BLOCK), BLOCK)
        return pltpu.make_async_copy(out.at[rows], updated.at[rows], sems.at[block])

    def one(block, carry):
        rows = pl.ds(pl.multiple_of(block * BLOCK, BLOCK), BLOCK)
        p = panel2[rows]
        left = jnp.concatenate([p, p[:, :PANEL]], axis=1)
        for n in range(COLS // 256):
            columns = pl.ds(n * 256, 256)
            out[rows, columns] = kept[rows, columns] - plain(left, x2[:, columns])
        write(block).start()
        return carry

    lax.fori_loop(0, BLOCKS, one, 0)

    def done(block, carry):
        write(block).wait()
        return carry

    lax.fori_loop(0, BLOCKS, done, 0)


def body(snapshots):
    dma = pltpu.SemaphoreType.DMA
    snapshots = pltpu.with_memory_space_constraint(snapshots, pltpu.HBM)
    kept, panel2, total, packed = pl.pallas_call(
        gather_kernel,
        name="panel_sums",
        out_shape=[
            pltpu.VMEM((ROWS, COLS), F32),
            pltpu.VMEM((ROWS, 2 * PANEL), BF16),
            pltpu.VMEM((PANEL, COLS), F32),
            pltpu.VMEM((PANEL, PANEL), F32),
        ],
        in_specs=[pl.BlockSpec(memory_space=pltpu.HBM)],
        out_specs=[pl.BlockSpec(memory_space=pltpu.VMEM)] * 4,
        scratch_shapes=[
            pltpu.VMEM((ROWS, PANEL), F32),
            pltpu.VMEM((ROWS, COLS), BF16),
            pltpu.VMEM((ROWS, COLS), BF16),
            pltpu.VMEM((PANEL, COLS), F32),
            pltpu.VMEM((PANEL, HALF), F32),
            pltpu.VMEM((PANEL, HALF), F32),
            pltpu.VMEM((CHIPS, PIECE, HALF), F32),
            pltpu.VMEM((PANEL, PANEL), F32),
            pltpu.VMEM((CHIPS, PIECE, PANEL), F32),
            pltpu.VMEM((PIECE, PANEL), F32),
            pltpu.VMEM((PIECE, PANEL), F32),
            pltpu.VMEM((PANEL, PANEL), F32),
            dma((BLOCKS,)), dma, dma((CHUNKS,)), dma((CHUNKS,)), dma, dma,
            dma((CHIPS,)), dma((CHIPS,)), dma((CHIPS,)), dma((CHIPS,)), dma, dma,
            dma((CHIPS,)), dma((CHIPS,)), dma, dma, dma((CHIPS,)), dma((CHIPS,)), dma((4,)), dma,
        ],
        compiler_params=pltpu.CompilerParams(
            collective_id=0, has_side_effects=True, vmem_limit_bytes=24 << 20
        ),
    )(snapshots)
    kept, panel2, total, packed = [
        pltpu.with_memory_space_constraint(a, pltpu.VMEM) for a in (kept, panel2, total, packed)
    ]
    return pl.pallas_call(
        apply_kernel,
        name="apply",
        out_shape=[
            jax.ShapeDtypeStruct((PANEL, PANEL), F32),
            jax.ShapeDtypeStruct((PANEL, COLS), F32),
            jax.ShapeDtypeStruct((ROWS, COLS), F32),
        ],
        in_specs=[pl.BlockSpec(memory_space=pltpu.VMEM)] * 4,
        out_specs=[
            pl.BlockSpec(memory_space=pltpu.VMEM),
            pl.BlockSpec(memory_space=pltpu.VMEM),
            pl.BlockSpec(memory_space=pl.ANY),
        ],
        scratch_shapes=[
            pltpu.VMEM((ROWS, COLS), F32),
            pltpu.VMEM((3 * PANEL, COLS), BF16),
            dma((BLOCKS,)),
        ],
        compiler_params=pltpu.CompilerParams(vmem_limit_bytes=24 << 20),
    )(kept, panel2, total, packed)


def solution(mesh):
    in_specs = (P("rows", "cols"),)
    out_specs = (P(), P(None, "cols"), P("rows", "cols"))
    return jax.shard_map(body, mesh=mesh, in_specs=in_specs, out_specs=out_specs, check_vma=False)
```

```python
import jax
import jax.numpy as jnp
from jax import lax
from jax.experimental import pallas as pl
from jax.experimental.pallas import tpu as pltpu
from jax.sharding import PartitionSpec as P

MESH = pl.DeviceIdType.MESH
F32 = jnp.float32
BF16 = jnp.bfloat16
PANEL = 128
ROWS = 2048
COLS = 1024
HALF = COLS // 2
CHIPS = 16
BLOCK = 256
BLOCKS = ROWS // BLOCK
CHUNK = 64
CHUNKS = ROWS // CHUNK
SIDE = CHUNKS // 2
DIRECT = 3
PER = BLOCK // CHUNK
PIECE = PANEL // CHIPS
TILE = 512
GROUP = 16
SIZE = 4
UNIT = 128
UNITS = ROWS // UNIT
NEAR = sorted(
    ((dz, dy) for dz in range(SIZE) for dy in range(SIZE) if dz or dy),
    key=lambda at: min(at[0], SIZE - at[0]) + min(at[1], SIZE - at[1]),
)
FAR = NEAR[::-1]


def slot(at):
    return at[0] * SIZE + at[1]


def split(value):
    high = value.astype(BF16)
    low = (value - high.astype(F32)).astype(BF16)
    return high, low


def cross(left, right):
    return lax.dot_general(left, right, (((0,), (0,)), ((), ())), preferred_element_type=F32)


def plain(left, right):
    return lax.dot_general(left, right, (((1,), (0,)), ((), ())), preferred_element_type=F32)


def inverse(value):
    guess = pl.reciprocal(value, approx=True)
    return guess * (2.0 - value * guess)


def triple(value):
    one = value.astype(BF16)
    rest = value - one.astype(F32)
    two = rest.astype(BF16)
    return one, two, (rest - two.astype(F32)).astype(BF16)


def cholesky(gram_ref, packed_ref):
    shape = (GROUP, PANEL)
    sub = lax.broadcasted_iota(jnp.int32, shape, 0)
    lane = lax.broadcasted_iota(jnp.int32, shape, 1)

    def across(value, k):
        return jnp.broadcast_to(value[k : k + 1, :], shape)

    count = PANEL // GROUP
    lefts = [gram_ref[n * GROUP : (n + 1) * GROUP, :] for n in range(count)]
    rights = [(lane == sub + n * GROUP).astype(F32) for n in range(count)]
    for n in range(count):
        base = n * GROUP
        top, side = lefts[n], rights[n]
        columns = [jnp.broadcast_to(top[:, base + k : base + k + 1], shape) for k in range(GROUP)]
        pivot = across(columns[0], 0)
        pivots = pivot
        for k in range(GROUP - 1):
            recip = inverse(pivot)
            link = across(columns[k + 1], k)
            pivot = across(columns[k + 1], k + 1) - (link * recip) * link
            pivots = jnp.where(sub > k, pivot, pivots)
            factor = jnp.where(sub > k, columns[k] * recip, 0.0)
            for j in range(k + 1, GROUP):
                columns[j] = columns[j] - factor * across(columns[j], k)
            top, side = top - factor * across(top, k), side - factor * across(side, k)
        scale = lax.rsqrt(pivots)
        scale = scale * (1.5 - 0.5 * pivots * scale * scale)
        top = jnp.where(lane >= sub + base, top * scale, 0.0)
        side = side * scale
        packed_ref[base : base + GROUP, :] = jnp.where(lane >= sub + base, top, side)
        if n + 1 < count:
            one, two, three = triple(jnp.concatenate([top, side], axis=1))
            update = cross(
                jnp.concatenate([v[:, :PANEL] for v in (one, one, two, two, one, three)], axis=0),
                jnp.concatenate([one, two, one, two, three, one], axis=0),
            )
            for m in range(n + 1, count):
                rows = update[m * GROUP : (m + 1) * GROUP]
                lefts[m] = lefts[m] - rows[:, :PANEL]
                rights[m] = rights[m] - rows[:, PANEL:]


def gather_kernel(
    snap, kept, panel2, total, packed,
    pbuf, high, low, wacc, swap, mine, parts, gram, gparts, gsum, gswap, gfull,
    load_sem, pload_sem, bs_send, bs_recv, ex_send, ex_recv, rs_send, rs_recv, ag_send, ag_recv,
    fx_send, fx_recv, gr_send, gr_recv, gx_send, gx_recv, ga_send, ga_recv, u_send, u_recv, meet,
):
    row = lax.axis_index("rows")
    col = lax.axis_index("cols")
    chip = row // 2
    core = row % 2
    partner = (chip * 2 + 1 - core, col)
    high_axis, low_axis = chip // SIZE, chip % SIZE

    def away(at):
        return ((high_axis + at[0]) % SIZE) * SIZE + (low_axis + at[1]) % SIZE

    def peer(at):
        return away(at) * 2 + core

    along_x = [(row, (col + step) % SIZE) for step in (1, SIZE - 1)]
    along_low = [(peer((0, step)), col) for step in (1, SIZE - 1)]
    along_high = [(peer((step, 0)), col) for step in (1, SIZE - 1)]
    rounds = [along_x + along_low, along_high, along_high]

    def announce(index):
        for other in rounds[index]:
            pl.semaphore_signal(meet.at[index], inc=1, device_id=other, device_id_type=MESH)

    def await_round(index):
        pl.semaphore_wait(meet.at[index], len(rounds[index]))

    greeted = along_x + along_low + along_high + [partner]
    barrier = pltpu.get_barrier_semaphore()
    for other in greeted:
        pl.semaphore_signal(barrier, inc=1, device_id=other, device_id_type=MESH)

    def load(block):
        rows = pl.ds(pl.multiple_of(block * BLOCK, BLOCK), BLOCK)
        return pltpu.make_async_copy(snap.at[rows], kept.at[rows], load_sem.at[block])

    panel_load = pltpu.make_async_copy(snap.at[:, pl.ds(0, PANEL)], pbuf, pload_sem)

    @pl.when(col == 0)
    def _():
        panel_load.start()

    def start_load(block, carry):
        load(block).start()
        return carry

    @pl.when(col != 0)
    def _():
        lax.fori_loop(0, BLOCKS, start_load, 0)

    pl.semaphore_wait(barrier, len(greeted))

    def chunk_rows(chunk):
        return pl.ds(pl.multiple_of(chunk * CHUNK, CHUNK), CHUNK)

    def relay(chunk, target):
        rows = chunk_rows(chunk)
        return pltpu.make_async_remote_copy(
            src_ref=pbuf.at[rows], dst_ref=pbuf.at[rows], send_sem=bs_send.at[chunk],
            recv_sem=bs_recv.at[chunk], device_id=(row, target), device_id_type=MESH,
        )

    def first(chunk, target, extra=0):
        rows = chunk_rows(chunk)
        return pltpu.make_async_remote_copy(
            src_ref=snap.at[rows, pl.ds(0, PANEL)], dst_ref=pbuf.at[rows], send_sem=bs_send.at[chunk + extra],
            recv_sem=bs_recv.at[chunk], device_id=(row, target), device_id_type=MESH,
        )

    @pl.when(col == 0)
    def _():
        def send(step, carry):
            first(step, 1).start()
            first(step + SIDE, 3).start()
            return carry

        def send_direct(step, carry):
            first(step + SIDE, 1, CHUNKS).start()
            first(step, 3, CHUNKS).start()
            return carry

        lax.fori_loop(0, SIDE, send, 0)
        lax.fori_loop(SIDE - DIRECT, SIDE, send_direct, 0)
        lax.fori_loop(0, BLOCKS, start_load, 0)
        announce(0)

    def block_rows(block):
        return pl.ds(pl.multiple_of(block * BLOCK, BLOCK), BLOCK)

    def widen(start, size):
        rows = pl.ds(pl.multiple_of(start, size), size)
        ph, plo = split(pbuf[rows])
        panel2[rows, :PANEL] = ph
        panel2[rows, PANEL:] = plo

    def prepare(block, carry):
        load(block).wait()
        rows = block_rows(block)
        sh, sl = split(kept[rows])
        high[rows] = sh
        low[rows] = sl
        return carry

    def accumulate(start, size):
        rows = pl.ds(pl.multiple_of(start, size), size)
        both = panel2[rows]
        for n in range(COLS // 256):
            columns = pl.ds(n * 256, 256)
            one = cross(both, high[rows, columns])
            two = cross(both[:, :PANEL], low[rows, columns])
            wacc[:, columns] += one[:PANEL] + one[PANEL:] + two

    def gram_piece(step):
        other = away(step)
        return pltpu.make_async_remote_copy(
            src_ref=gram.at[pl.ds(pl.multiple_of(other * PIECE, PIECE), PIECE)], dst_ref=gparts.at[chip],
            send_sem=gr_send.at[slot(step)], recv_sem=gr_recv.at[chip], device_id=(peer(step), col), device_id_type=MESH,
        )

    def gram_arrived(step):
        other = away(step)
        return pltpu.make_async_remote_copy(
            src_ref=gram.at[pl.ds(0, PIECE)], dst_ref=gparts.at[other],
            send_sem=gr_send.at[slot(step)], recv_sem=gr_recv.at[other], device_id=(peer(step), col), device_id_type=MESH,
        )

    @pl.when(col == 0)
    def _():
        panel_load.wait()

        def one(block, carry):
            widen(block * BLOCK, BLOCK)
            return carry

        lax.fori_loop(0, BLOCKS, one, 0)
        full = cross(panel2[...], panel2[...])
        gram[...] = full[:PANEL, :PANEL] + (full[:PANEL, PANEL:] + full[PANEL:, :PANEL]) + full[PANEL:, PANEL:]

        await_round(0)
        announce(1)
        await_round(1)
        announce(2)
        await_round(2)
        for at in FAR:
            gram_piece(at).start()
        gparts[chip] = gram[pl.ds(pl.multiple_of(chip * PIECE, PIECE), PIECE)]

    wacc[...] = jnp.zeros_like(wacc)

    @pl.when(col == 0)
    def _():
        lax.fori_loop(0, BLOCKS, prepare, 0)

        def one(block, carry):
            accumulate(block * BLOCK, BLOCK)
            return carry

        lax.fori_loop(0, BLOCKS, one, 0)

    @pl.when(col != 0)
    def _():
        def pass_on(step):
            straight = (step + jnp.where(col == 3, SIDE, 0)) % CHUNKS
            chunk = jnp.where(col == 2, (step % 2) * SIDE + step // 2, straight)
            onward = jnp.where(chunk < SIDE, col + 1, col - 1)
            relay(chunk, 0).wait_recv()

            @pl.when((onward > 0) & (onward < 4) & ((col != 2) | (chunk % SIDE < SIDE - DIRECT)))
            def _():
                relay(chunk, onward).start()

        def work(index):
            straight = (index + jnp.where(col == 3, UNITS // 2, 0)) % UNITS
            unit = jnp.where(col == 2, (index % 2) * (UNITS // 2) + index // 2, straight)
            widen(unit * UNIT, UNIT)
            accumulate(unit * UNIT, UNIT)

        def early(step, carry):
            pass_on(step)
            prepare(step, 0)
            return carry

        def middle(step, carry):
            pass_on(step)
            work(step - BLOCKS)
            return carry

        def late(pair, carry):
            pass_on(2 * pair)
            work(pair - 1)
            pass_on(2 * pair + 1)
            return carry

        announce(0)
        lax.fori_loop(0, 2, early, 0)
        await_round(0)
        announce(1)
        lax.fori_loop(2, 4, early, 0)
        await_round(1)
        announce(2)
        lax.fori_loop(4, 6, early, 0)
        await_round(2)
        lax.fori_loop(6, BLOCKS, early, 0)
        lax.fori_loop(BLOCKS, 15, middle, 0)
        pass_on(15)
        lax.fori_loop(8, UNITS, late, 0)
        work(UNITS - 1)

    exchange = pltpu.make_async_remote_copy(
        src_ref=wacc.at[:, pl.ds(pl.multiple_of((1 - core) * HALF, HALF), HALF)], dst_ref=swap,
        send_sem=ex_send, recv_sem=ex_recv, device_id=partner, device_id_type=MESH,
    )
    exchange.start()

    gram_swap = pltpu.make_async_remote_copy(
        src_ref=gsum, dst_ref=gswap, send_sem=gx_send, recv_sem=gx_recv, device_id=partner, device_id_type=MESH,
    )

    def gram_gather(step):
        rows = pl.ds(pl.multiple_of(chip * PIECE, PIECE), PIECE)
        return pltpu.make_async_remote_copy(
            src_ref=gfull.at[rows], dst_ref=gfull.at[rows],
            send_sem=ga_send.at[slot(step)], recv_sem=ga_recv.at[chip], device_id=(peer(step), col), device_id_type=MESH,
        )

    def gram_gathered(step):
        other = away(step)
        rows = pl.ds(pl.multiple_of(other * PIECE, PIECE), PIECE)
        return pltpu.make_async_remote_copy(
            src_ref=gfull.at[rows], dst_ref=gfull.at[rows],
            send_sem=ga_send.at[slot(step)], recv_sem=ga_recv.at[other], device_id=(peer(step), col), device_id_type=MESH,
        )

    @pl.when(col == 0)
    def _():
        for at in NEAR:
            gram_arrived(at).wait_recv()
        gsum[...] = jnp.sum(gparts[...], axis=0)
        gram_swap.start()
        gram_swap.wait()
        gfull[pl.ds(pl.multiple_of(chip * PIECE, PIECE), PIECE)] = gsum[...] + gswap[...]

        for at in FAR:
            gram_gather(at).start()

    exchange.wait()
    mine[...] = wacc[:, pl.ds(pl.multiple_of(core * HALF, HALF), HALF)] + swap[...]

    def scatter(step):
        other = away(step)
        return pltpu.make_async_remote_copy(
            src_ref=mine.at[pl.ds(pl.multiple_of(other * PIECE, PIECE), PIECE)], dst_ref=parts.at[chip],
            send_sem=rs_send.at[slot(step)], recv_sem=rs_recv.at[chip], device_id=(peer(step), col), device_id_type=MESH,
        )

    def scattered(step):
        other = away(step)
        return pltpu.make_async_remote_copy(
            src_ref=mine.at[pl.ds(0, PIECE)], dst_ref=parts.at[other],
            send_sem=rs_send.at[slot(step)], recv_sem=rs_recv.at[other], device_id=(peer(step), col), device_id_type=MESH,
        )

    for at in FAR:
        scatter(at).start()
    parts[chip] = mine[pl.ds(pl.multiple_of(chip * PIECE, PIECE), PIECE)]

    def send_packed(target):
        return pltpu.make_async_remote_copy(
            src_ref=packed, dst_ref=packed, send_sem=u_send.at[target], recv_sem=u_recv,
            device_id=(row, target), device_id_type=MESH,
        )

    @pl.when(col == 0)
    def _():
        for at in NEAR:
            gram_gathered(at).wait_recv()
        cholesky(gfull, packed)
        for target in (2, 1, 3):
            send_packed(target).start()

    for at in NEAR:
        scattered(at).wait_recv()
    half = pl.ds(pl.multiple_of(core * HALF, HALF), HALF)
    own = pl.ds(pl.multiple_of(chip * PIECE, PIECE), PIECE)
    total[own, half] = jnp.sum(parts[...], axis=0)

    def gather(step):
        return pltpu.make_async_remote_copy(
            src_ref=total.at[own, half], dst_ref=total.at[own, half],
            send_sem=ag_send.at[slot(step)], recv_sem=ag_recv.at[chip], device_id=(peer(step), col), device_id_type=MESH,
        )

    def gathered(step):
        other = away(step)
        rows = pl.ds(pl.multiple_of(other * PIECE, PIECE), PIECE)
        return pltpu.make_async_remote_copy(
            src_ref=total.at[rows, half], dst_ref=total.at[rows, half],
            send_sem=ag_send.at[slot(step)], recv_sem=ag_recv.at[other], device_id=(peer(step), col), device_id_type=MESH,
        )

    def onward(owner, columns):
        rows = pl.ds(pl.multiple_of(owner * PIECE, PIECE), PIECE)
        return pltpu.make_async_remote_copy(
            src_ref=total.at[rows, columns], dst_ref=total.at[rows, columns], send_sem=fx_send.at[owner],
            recv_sem=fx_recv.at[owner], device_id=partner, device_id_type=MESH,
        )

    for at in FAR:
        gather(at).start()
    onward(chip, half).start()
    for at in NEAR:
        gathered(at).wait_recv()
        onward(away(at), half).start()
    other_half = pl.ds(pl.multiple_of((1 - core) * HALF, HALF), HALF)

    for at in NEAR:
        scatter(at).wait_send()
        gather(at).wait_send()

    @pl.when(col == 0)
    def _():
        for at in NEAR:
            gram_piece(at).wait_send()
            gram_gather(at).wait_send()
        for target in (2, 1, 3):
            send_packed(target).wait_send()

        def sent(chunk, carry):
            first(chunk, 1).wait_send()
            return carry

        lax.fori_loop(0, CHUNKS, sent, 0)

        def sent_direct(step, carry):
            first(step + SIDE, 1, CHUNKS).wait_send()
            first(step, 3, CHUNKS).wait_send()
            return carry

        lax.fori_loop(SIDE - DIRECT, SIDE, sent_direct, 0)

    def sent_on(chunk, carry):
        relay(chunk, 0).wait_send()
        return carry

    @pl.when(col == 1)
    def _():
        lax.fori_loop(0, SIDE, sent_on, 0)

    @pl.when(col == 2)
    def _():
        lax.fori_loop(0, SIDE - DIRECT, sent_on, 0)
        lax.fori_loop(SIDE, CHUNKS - DIRECT, sent_on, 0)

    @pl.when(col == 3)
    def _():
        lax.fori_loop(SIDE, CHUNKS, sent_on, 0)

    @pl.when(col != 0)
    def _():
        send_packed(0).wait_recv()

    def finish(owner, carry):
        onward(owner, half).wait_send()
        onward(owner, other_half).wait_recv()
        return carry

    lax.fori_loop(0, CHIPS, finish, 0)


def apply_kernel(kept, panel2, total, packed, factor, coupling, updated, out, x2, sems):
    both = packed[...]
    sub = lax.broadcasted_iota(jnp.int32, (PANEL, PANEL), 0)
    lane = lax.broadcasted_iota(jnp.int32, (PANEL, PANEL), 1)
    factor[...] = jnp.where(lane >= sub, both, 0.0) * (1.0 / 256.0)
    lower = jnp.where(lane < sub, both, jnp.where(lane == sub, 1.0 / both, 0.0))
    lh, ll = split(lower)
    th, tl = split(lower.T)
    to_coupling = jnp.concatenate([lh, ll, lh], axis=1)
    to_weights = jnp.concatenate([th, tl, th], axis=1)
    copies = []
    for n in range(COLS // TILE):
        columns = pl.ds(n * TILE, TILE)
        wh, wl = split(total[:, columns])
        c = plain(to_coupling, jnp.concatenate([wh, wh, wl], axis=0))
        coupling[:, columns] = c
        ch, cl = split(c)
        xh, xl = split(plain(to_weights, jnp.concatenate([ch, ch, cl], axis=0)))
        x2[:, columns] = jnp.concatenate([xh, xh, xl], axis=0)
        for block in range(BLOCKS):
            rows = pl.ds(block * BLOCK, BLOCK)
            p = panel2[rows]
            left = jnp.concatenate([p, p[:, :PANEL]], axis=1)
            out[rows, columns] = kept[rows, columns] - plain(left, x2[:, columns])
            copy = pltpu.make_async_copy(
                out.at[rows, columns], updated.at[rows, columns], sems.at[n * BLOCKS + block]
            )
            copy.start()
            copies.append(copy)
    for copy in copies:
        copy.wait()


def body(snapshots):
    dma = pltpu.SemaphoreType.DMA
    snapshots = pltpu.with_memory_space_constraint(snapshots, pltpu.HBM)
    kept, panel2, total, packed = pl.pallas_call(
        gather_kernel,
        name="panel_sums",
        out_shape=[
            pltpu.VMEM((ROWS, COLS), F32),
            pltpu.VMEM((ROWS, 2 * PANEL), BF16),
            pltpu.VMEM((PANEL, COLS), F32),
            pltpu.VMEM((PANEL, PANEL), F32),
        ],
        in_specs=[pl.BlockSpec(memory_space=pltpu.HBM)],
        out_specs=[pl.BlockSpec(memory_space=pltpu.VMEM)] * 4,
        scratch_shapes=[
            pltpu.VMEM((ROWS, PANEL), F32),
            pltpu.VMEM((ROWS, COLS), BF16),
            pltpu.VMEM((ROWS, COLS), BF16),
            pltpu.VMEM((PANEL, COLS), F32),
            pltpu.VMEM((PANEL, HALF), F32),
            pltpu.VMEM((PANEL, HALF), F32),
            pltpu.VMEM((CHIPS, PIECE, HALF), F32),
            pltpu.VMEM((PANEL, PANEL), F32),
            pltpu.VMEM((CHIPS, PIECE, PANEL), F32),
            pltpu.VMEM((PIECE, PANEL), F32),
            pltpu.VMEM((PIECE, PANEL), F32),
            pltpu.VMEM((PANEL, PANEL), F32),
            dma((BLOCKS,)), dma, dma((2 * CHUNKS,)), dma((CHUNKS,)), dma, dma,
            dma((CHIPS,)), dma((CHIPS,)), dma((CHIPS,)), dma((CHIPS,)), dma((CHIPS,)), dma((CHIPS,)),
            dma((CHIPS,)), dma((CHIPS,)), dma, dma, dma((CHIPS,)), dma((CHIPS,)), dma((4,)), dma,
            pltpu.SemaphoreType.REGULAR((3,)),
        ],
        compiler_params=pltpu.CompilerParams(
            collective_id=0, has_side_effects=True, vmem_limit_bytes=24 << 20
        ),
    )(snapshots)
    kept, panel2, total, packed = [
        pltpu.with_memory_space_constraint(a, pltpu.VMEM) for a in (kept, panel2, total, packed)
    ]
    return pl.pallas_call(
        apply_kernel,
        name="apply",
        out_shape=[
            jax.ShapeDtypeStruct((PANEL, PANEL), F32),
            jax.ShapeDtypeStruct((PANEL, COLS), F32),
            jax.ShapeDtypeStruct((ROWS, COLS), F32),
        ],
        in_specs=[pl.BlockSpec(memory_space=pltpu.VMEM)] * 4,
        out_specs=[
            pl.BlockSpec(memory_space=pltpu.VMEM),
            pl.BlockSpec(memory_space=pltpu.VMEM),
            pl.BlockSpec(memory_space=pl.ANY),
        ],
        scratch_shapes=[
            pltpu.VMEM((ROWS, COLS), F32),
            pltpu.VMEM((3 * PANEL, COLS), BF16),
            dma((BLOCKS * COLS // TILE,)),
        ],
        compiler_params=pltpu.CompilerParams(vmem_limit_bytes=24 << 20),
    )(kept, panel2, total, packed)


def solution(mesh):
    in_specs = (P("rows", "cols"),)
    out_specs = (P(), P(None, "cols"), P("rows", "cols"))
    return jax.shard_map(body, mesh=mesh, in_specs=in_specs, out_specs=out_specs, check_vma=False)
```

```python
import jax
import jax.numpy as jnp
from jax import lax
from jax.experimental import pallas as pl
from jax.experimental.pallas import tpu as pltpu
from jax.sharding import PartitionSpec as P

MESH = pl.DeviceIdType.MESH
F32 = jnp.float32
BF16 = jnp.bfloat16
PANEL = 128
ROWS = 2048
COLS = 1024
HALF = COLS // 2
CHIPS = 16
BLOCK = 256
BLOCKS = ROWS // BLOCK
CHUNK = 64
CHUNKS = ROWS // CHUNK
RIGHT = 16
LEFT = CHUNKS - RIGHT
HEAD = RIGHT - LEFT
RIGHT_DIRECT = 6
LEFT_DIRECT = 8
PER = BLOCK // CHUNK
PIECE = PANEL // CHIPS
TILE = 512
GROUP = 16
SIZE = 4
UNIT = 128
UNITS = ROWS // UNIT
NEAR = sorted(
    ((dz, dy) for dz in range(SIZE) for dy in range(SIZE) if dz or dy),
    key=lambda at: min(at[0], SIZE - at[0]) + min(at[1], SIZE - at[1]),
)
FAR = NEAR[::-1]


def slot(at):
    return at[0] * SIZE + at[1]


def split(value):
    high = value.astype(BF16)
    low = (value - high.astype(F32)).astype(BF16)
    return high, low


def cross(left, right):
    return lax.dot_general(left, right, (((0,), (0,)), ((), ())), preferred_element_type=F32)


def plain(left, right):
    return lax.dot_general(left, right, (((1,), (0,)), ((), ())), preferred_element_type=F32)


def inverse(value):
    guess = pl.reciprocal(value, approx=True)
    return guess * (2.0 - value * guess)


def triple(value):
    one = value.astype(BF16)
    rest = value - one.astype(F32)
    two = rest.astype(BF16)
    return one, two, (rest - two.astype(F32)).astype(BF16)


def cholesky(gram_ref, packed_ref):
    shape = (GROUP, PANEL)
    sub = lax.broadcasted_iota(jnp.int32, shape, 0)
    lane = lax.broadcasted_iota(jnp.int32, shape, 1)

    def across(value, k):
        return jnp.broadcast_to(value[k : k + 1, :], shape)

    count = PANEL // GROUP
    lefts = [gram_ref[n * GROUP : (n + 1) * GROUP, :] for n in range(count)]
    rights = [(lane == sub + n * GROUP).astype(F32) for n in range(count)]
    for n in range(count):
        base = n * GROUP
        top, side = lefts[n], rights[n]
        columns = [jnp.broadcast_to(top[:, base + k : base + k + 1], shape) for k in range(GROUP)]
        pivot = across(columns[0], 0)
        pivots = pivot
        for k in range(GROUP - 1):
            recip = inverse(pivot)
            link = across(columns[k + 1], k)
            pivot = across(columns[k + 1], k + 1) - (link * recip) * link
            pivots = jnp.where(sub > k, pivot, pivots)
            factor = jnp.where(sub > k, columns[k] * recip, 0.0)
            for j in range(k + 1, GROUP):
                columns[j] = columns[j] - factor * across(columns[j], k)
            top, side = top - factor * across(top, k), side - factor * across(side, k)
        scale = lax.rsqrt(pivots)
        scale = scale * (1.5 - 0.5 * pivots * scale * scale)
        top = jnp.where(lane >= sub + base, top * scale, 0.0)
        side = side * scale
        packed_ref[base : base + GROUP, :] = jnp.where(lane >= sub + base, top, side)
        if n + 1 < count:
            one, two, three = triple(jnp.concatenate([top, side], axis=1))
            update = cross(
                jnp.concatenate([v[:, :PANEL] for v in (one, one, two, two, one, three)], axis=0),
                jnp.concatenate([one, two, one, two, three, one], axis=0),
            )
            for m in range(n + 1, count):
                rows = update[m * GROUP : (m + 1) * GROUP]
                lefts[m] = lefts[m] - rows[:, :PANEL]
                rights[m] = rights[m] - rows[:, PANEL:]


def gather_kernel(
    snap, kept, panel2, total, packed,
    pbuf, high, low, wacc, swap, mine, parts, gram, gparts, gsum, gswap, gfull,
    load_sem, pload_sem, bs_send, bs_recv, ex_send, ex_recv, rs_send, rs_recv, ag_send, ag_recv,
    fx_send, fx_recv, gr_send, gr_recv, gx_send, gx_recv, ga_send, ga_recv, u_send, u_recv, meet,
):
    row = lax.axis_index("rows")
    col = lax.axis_index("cols")
    chip = row // 2
    core = row % 2
    partner = (chip * 2 + 1 - core, col)
    high_axis, low_axis = chip // SIZE, chip % SIZE

    def away(at):
        return ((high_axis + at[0]) % SIZE) * SIZE + (low_axis + at[1]) % SIZE

    def peer(at):
        return away(at) * 2 + core

    along_x = [(row, (col + step) % SIZE) for step in (1, SIZE - 1)]
    along_low = [(peer((0, step)), col) for step in (1, SIZE - 1)]
    along_high = [(peer((step, 0)), col) for step in (1, SIZE - 1)]
    rounds = [along_x + along_low, along_high, along_high]

    def announce(index):
        for other in rounds[index]:
            pl.semaphore_signal(meet.at[index], inc=1, device_id=other, device_id_type=MESH)

    def await_round(index):
        pl.semaphore_wait(meet.at[index], len(rounds[index]))

    greeted = along_x + along_low + along_high + [partner]
    barrier = pltpu.get_barrier_semaphore()
    for other in greeted:
        pl.semaphore_signal(barrier, inc=1, device_id=other, device_id_type=MESH)

    def load(block):
        rows = pl.ds(pl.multiple_of(block * BLOCK, BLOCK), BLOCK)
        return pltpu.make_async_copy(snap.at[rows], kept.at[rows], load_sem.at[block])

    panel_load = pltpu.make_async_copy(snap.at[:, pl.ds(0, PANEL)], pbuf, pload_sem)

    @pl.when(col == 0)
    def _():
        panel_load.start()

    def start_load(block, carry):
        load(block).start()
        return carry

    @pl.when(col != 0)
    def _():
        lax.fori_loop(0, BLOCKS, start_load, 0)

    pl.semaphore_wait(barrier, len(greeted))

    def chunk_rows(chunk):
        return pl.ds(pl.multiple_of(chunk * CHUNK, CHUNK), CHUNK)

    def relay(chunk, target):
        rows = chunk_rows(chunk)
        return pltpu.make_async_remote_copy(
            src_ref=pbuf.at[rows], dst_ref=pbuf.at[rows], send_sem=bs_send.at[chunk],
            recv_sem=bs_recv.at[chunk], device_id=(row, target), device_id_type=MESH,
        )

    def first(chunk, target, extra=0):
        rows = chunk_rows(chunk)
        return pltpu.make_async_remote_copy(
            src_ref=pbuf.at[rows], dst_ref=pbuf.at[rows], send_sem=bs_send.at[chunk + extra],
            recv_sem=bs_recv.at[chunk], device_id=(row, target), device_id_type=MESH,
        )

    @pl.when(col == 0)
    def _():
        def send_right(step, carry):
            first(step, 1).start()
            return carry

        def send(step, carry):
            first(step + HEAD, 1).start()
            first(step + RIGHT, 3).start()
            return carry

        panel_load.wait()
        lax.fori_loop(0, HEAD, send_right, 0)
        lax.fori_loop(0, LEFT, send, 0)
        for step in range(max(RIGHT_DIRECT, LEFT_DIRECT)):
            if step < LEFT_DIRECT:
                first(CHUNKS - LEFT_DIRECT + step, 1, CHUNKS).start()
            if step < RIGHT_DIRECT:
                first(RIGHT - RIGHT_DIRECT + step, 3, CHUNKS).start()
        lax.fori_loop(0, BLOCKS, start_load, 0)
        announce(0)

    def block_rows(block):
        return pl.ds(pl.multiple_of(block * BLOCK, BLOCK), BLOCK)

    def widen(start, size):
        rows = pl.ds(pl.multiple_of(start, size), size)
        ph, plo = split(pbuf[rows])
        panel2[rows, :PANEL] = ph
        panel2[rows, PANEL:] = plo

    def prepare(block, carry):
        load(block).wait()
        rows = block_rows(block)
        sh, sl = split(kept[rows])
        high[rows] = sh
        low[rows] = sl
        return carry

    def accumulate(start, size):
        rows = pl.ds(pl.multiple_of(start, size), size)
        both = panel2[rows]
        for n in range(COLS // 256):
            columns = pl.ds(n * 256, 256)
            one = cross(both, high[rows, columns])
            two = cross(both[:, :PANEL], low[rows, columns])
            wacc[:, columns] += one[:PANEL] + one[PANEL:] + two

    def gram_piece(step):
        other = away(step)
        return pltpu.make_async_remote_copy(
            src_ref=gram.at[pl.ds(pl.multiple_of(other * PIECE, PIECE), PIECE)], dst_ref=gparts.at[chip],
            send_sem=gr_send.at[slot(step)], recv_sem=gr_recv.at[chip], device_id=(peer(step), col), device_id_type=MESH,
        )

    def gram_arrived(step):
        other = away(step)
        return pltpu.make_async_remote_copy(
            src_ref=gram.at[pl.ds(0, PIECE)], dst_ref=gparts.at[other],
            send_sem=gr_send.at[slot(step)], recv_sem=gr_recv.at[other], device_id=(peer(step), col), device_id_type=MESH,
        )

    @pl.when(col == 0)
    def _():

        def one(block, carry):
            widen(block * BLOCK, BLOCK)
            return carry

        lax.fori_loop(0, BLOCKS, one, 0)
        full = cross(panel2[...], panel2[...])
        gram[...] = full[:PANEL, :PANEL] + (full[:PANEL, PANEL:] + full[PANEL:, :PANEL]) + full[PANEL:, PANEL:]

        await_round(0)
        announce(1)
        await_round(1)
        announce(2)
        await_round(2)
        for at in FAR:
            gram_piece(at).start()
        gparts[chip] = gram[pl.ds(pl.multiple_of(chip * PIECE, PIECE), PIECE)]

    wacc[...] = jnp.zeros_like(wacc)

    @pl.when(col == 0)
    def _():
        lax.fori_loop(0, BLOCKS, prepare, 0)

        def one(block, carry):
            accumulate(block * BLOCK, BLOCK)
            return carry

        lax.fori_loop(0, BLOCKS, one, 0)

    @pl.when(col != 0)
    def _():
        def ordered(step, right, head, count):
            turn = jnp.maximum(step - head, 0)
            both_ways = jnp.where(step < head, step, jnp.where(turn % 2 == 0, head, right) + turn // 2)
            straight = (step + jnp.where(col == 3, right, 0)) % count
            return jnp.where(col == 2, both_ways, straight)

        def pass_on(step):
            chunk = ordered(step, RIGHT, HEAD, CHUNKS)
            onward = jnp.where(chunk < RIGHT, col + 1, col - 1)
            shared = jnp.where(chunk < RIGHT, RIGHT - RIGHT_DIRECT, CHUNKS - LEFT_DIRECT)
            limit = jnp.where(col == 2, shared, CHUNKS)
            relay(chunk, 0).wait_recv()

            @pl.when((onward > 0) & (onward < 4) & (chunk < limit))
            def _():
                relay(chunk, onward).start()

        def work(index):
            unit = ordered(index, RIGHT // 2, HEAD // 2, UNITS)
            widen(unit * UNIT, UNIT)
            accumulate(unit * UNIT, UNIT)

        def early(step, carry):
            pass_on(step)
            prepare(step, 0)
            return carry

        def middle(step, carry):
            pass_on(step)
            work(step - BLOCKS)
            return carry

        def late(pair, carry):
            pass_on(2 * pair)
            work(pair - 1)
            pass_on(2 * pair + 1)
            return carry

        announce(0)

        lax.fori_loop(0, 2, early, 0)
        await_round(0)
        announce(1)
        lax.fori_loop(2, 4, early, 0)
        await_round(1)
        announce(2)
        lax.fori_loop(4, 6, early, 0)
        await_round(2)
        lax.fori_loop(6, BLOCKS, early, 0)
        lax.fori_loop(BLOCKS, 15, middle, 0)
        pass_on(15)
        lax.fori_loop(8, UNITS, late, 0)
        work(UNITS - 1)

    exchange = pltpu.make_async_remote_copy(
        src_ref=wacc.at[:, pl.ds(pl.multiple_of((1 - core) * HALF, HALF), HALF)], dst_ref=swap,
        send_sem=ex_send, recv_sem=ex_recv, device_id=partner, device_id_type=MESH,
    )
    exchange.start()

    gram_swap = pltpu.make_async_remote_copy(
        src_ref=gsum, dst_ref=gswap, send_sem=gx_send, recv_sem=gx_recv, device_id=partner, device_id_type=MESH,
    )

    def gram_gather(step):
        rows = pl.ds(pl.multiple_of(chip * PIECE, PIECE), PIECE)
        return pltpu.make_async_remote_copy(
            src_ref=gfull.at[rows], dst_ref=gfull.at[rows],
            send_sem=ga_send.at[slot(step)], recv_sem=ga_recv.at[chip], device_id=(peer(step), col), device_id_type=MESH,
        )

    def gram_gathered(step):
        other = away(step)
        rows = pl.ds(pl.multiple_of(other * PIECE, PIECE), PIECE)
        return pltpu.make_async_remote_copy(
            src_ref=gfull.at[rows], dst_ref=gfull.at[rows],
            send_sem=ga_send.at[slot(step)], recv_sem=ga_recv.at[other], device_id=(peer(step), col), device_id_type=MESH,
        )

    @pl.when(col == 0)
    def _():
        for at in NEAR:
            gram_arrived(at).wait_recv()
        gsum[...] = jnp.sum(gparts[...], axis=0)
        gram_swap.start()
        gram_swap.wait()
        gfull[pl.ds(pl.multiple_of(chip * PIECE, PIECE), PIECE)] = gsum[...] + gswap[...]

        for at in FAR:
            gram_gather(at).start()

    exchange.wait()
    mine[...] = wacc[:, pl.ds(pl.multiple_of(core * HALF, HALF), HALF)] + swap[...]

    def scatter(step):
        other = away(step)
        return pltpu.make_async_remote_copy(
            src_ref=mine.at[pl.ds(pl.multiple_of(other * PIECE, PIECE), PIECE)], dst_ref=parts.at[chip],
            send_sem=rs_send.at[slot(step)], recv_sem=rs_recv.at[chip], device_id=(peer(step), col), device_id_type=MESH,
        )

    def scattered(step):
        other = away(step)
        return pltpu.make_async_remote_copy(
            src_ref=mine.at[pl.ds(0, PIECE)], dst_ref=parts.at[other],
            send_sem=rs_send.at[slot(step)], recv_sem=rs_recv.at[other], device_id=(peer(step), col), device_id_type=MESH,
        )

    for at in FAR:
        scatter(at).start()
    parts[chip] = mine[pl.ds(pl.multiple_of(chip * PIECE, PIECE), PIECE)]

    def sent_on(chunk, carry):
        relay(chunk, 0).wait_send()
        return carry

    @pl.when(col == 1)
    def _():
        lax.fori_loop(0, RIGHT, sent_on, 0)

    @pl.when(col == 2)
    def _():
        lax.fori_loop(0, RIGHT - RIGHT_DIRECT, sent_on, 0)
        lax.fori_loop(RIGHT, CHUNKS - LEFT_DIRECT, sent_on, 0)

    @pl.when(col == 3)
    def _():
        lax.fori_loop(RIGHT, CHUNKS, sent_on, 0)

    def send_packed(target):
        return pltpu.make_async_remote_copy(
            src_ref=packed, dst_ref=packed, send_sem=u_send.at[target], recv_sem=u_recv,
            device_id=(row, target), device_id_type=MESH,
        )

    @pl.when(col == 0)
    def _():
        for at in NEAR:
            gram_gathered(at).wait_recv()
        cholesky(gfull, packed)
        for target in (2, 1, 3):
            send_packed(target).start()

        def sent(chunk, carry):
            first(chunk, 1).wait_send()
            return carry

        lax.fori_loop(0, CHUNKS, sent, 0)

        for step in range(LEFT_DIRECT):
            first(CHUNKS - LEFT_DIRECT + step, 1, CHUNKS).wait_send()
        for step in range(RIGHT_DIRECT):
            first(RIGHT - RIGHT_DIRECT + step, 3, CHUNKS).wait_send()

    for at in NEAR:
        scattered(at).wait_recv()
    half = pl.ds(pl.multiple_of(core * HALF, HALF), HALF)
    own = pl.ds(pl.multiple_of(chip * PIECE, PIECE), PIECE)
    total[own, half] = jnp.sum(parts[...], axis=0)

    def gather(step):
        return pltpu.make_async_remote_copy(
            src_ref=total.at[own, half], dst_ref=total.at[own, half],
            send_sem=ag_send.at[slot(step)], recv_sem=ag_recv.at[chip], device_id=(peer(step), col), device_id_type=MESH,
        )

    def gathered(step):
        other = away(step)
        rows = pl.ds(pl.multiple_of(other * PIECE, PIECE), PIECE)
        return pltpu.make_async_remote_copy(
            src_ref=total.at[rows, half], dst_ref=total.at[rows, half],
            send_sem=ag_send.at[slot(step)], recv_sem=ag_recv.at[other], device_id=(peer(step), col), device_id_type=MESH,
        )

    def onward(owner, columns):
        rows = pl.ds(pl.multiple_of(owner * PIECE, PIECE), PIECE)
        return pltpu.make_async_remote_copy(
            src_ref=total.at[rows, columns], dst_ref=total.at[rows, columns], send_sem=fx_send.at[owner],
            recv_sem=fx_recv.at[owner], device_id=partner, device_id_type=MESH,
        )

    for at in FAR:
        gather(at).start()
    onward(chip, half).start()
    for at in NEAR:
        scatter(at).wait_send()
    for at in NEAR:
        gathered(at).wait_recv()
        onward(away(at), half).start()
    other_half = pl.ds(pl.multiple_of((1 - core) * HALF, HALF), HALF)

    for at in NEAR:
        gather(at).wait_send()

    @pl.when(col == 0)
    def _():
        for at in NEAR:
            gram_piece(at).wait_send()
            gram_gather(at).wait_send()
        for target in (2, 1, 3):
            send_packed(target).wait_send()

    @pl.when(col != 0)
    def _():
        send_packed(0).wait_recv()

    def finish(owner, carry):
        onward(owner, half).wait_send()
        onward(owner, other_half).wait_recv()
        return carry

    lax.fori_loop(0, CHIPS, finish, 0)


def apply_kernel(kept, panel2, total, packed, factor, coupling, updated, out, x2, sems):
    both = packed[...]
    sub = lax.broadcasted_iota(jnp.int32, (PANEL, PANEL), 0)
    lane = lax.broadcasted_iota(jnp.int32, (PANEL, PANEL), 1)
    factor[...] = jnp.where(lane >= sub, both, 0.0) * (1.0 / 256.0)
    lower = jnp.where(lane < sub, both, jnp.where(lane == sub, 1.0 / both, 0.0))
    lh, ll = split(lower)
    th, tl = split(lower.T)
    to_coupling = jnp.concatenate([lh, ll, lh], axis=1)
    to_weights = jnp.concatenate([th, tl, th], axis=1)
    copies = []
    for n in range(COLS // TILE):
        columns = pl.ds(n * TILE, TILE)
        wh, wl = split(total[:, columns])
        c = plain(to_coupling, jnp.concatenate([wh, wh, wl], axis=0))
        coupling[:, columns] = c
        ch, cl = split(c)
        xh, xl = split(plain(to_weights, jnp.concatenate([ch, ch, cl], axis=0)))
        x2[:, columns] = jnp.concatenate([xh, xh, xl], axis=0)
        for block in range(BLOCKS):
            rows = pl.ds(block * BLOCK, BLOCK)
            p = panel2[rows]
            left = jnp.concatenate([p, p[:, :PANEL]], axis=1)
            out[rows, columns] = kept[rows, columns] - plain(left, x2[:, columns])
            copy = pltpu.make_async_copy(
                out.at[rows, columns], updated.at[rows, columns], sems.at[n * BLOCKS + block]
            )
            copy.start()
            copies.append(copy)
    for copy in copies:
        copy.wait()


def body(snapshots):
    dma = pltpu.SemaphoreType.DMA
    snapshots = pltpu.with_memory_space_constraint(snapshots, pltpu.HBM)
    kept, panel2, total, packed = pl.pallas_call(
        gather_kernel,
        name="panel_sums",
        out_shape=[
            pltpu.VMEM((ROWS, COLS), F32),
            pltpu.VMEM((ROWS, 2 * PANEL), BF16),
            pltpu.VMEM((PANEL, COLS), F32),
            pltpu.VMEM((PANEL, PANEL), F32),
        ],
        in_specs=[pl.BlockSpec(memory_space=pltpu.HBM)],
        out_specs=[pl.BlockSpec(memory_space=pltpu.VMEM)] * 4,
        scratch_shapes=[
            pltpu.VMEM((ROWS, PANEL), F32),
            pltpu.VMEM((ROWS, COLS), BF16),
            pltpu.VMEM((ROWS, COLS), BF16),
            pltpu.VMEM((PANEL, COLS), F32),
            pltpu.VMEM((PANEL, HALF), F32),
            pltpu.VMEM((PANEL, HALF), F32),
            pltpu.VMEM((CHIPS, PIECE, HALF), F32),
            pltpu.VMEM((PANEL, PANEL), F32),
            pltpu.VMEM((CHIPS, PIECE, PANEL), F32),
            pltpu.VMEM((PIECE, PANEL), F32),
            pltpu.VMEM((PIECE, PANEL), F32),
            pltpu.VMEM((PANEL, PANEL), F32),
            dma((BLOCKS,)), dma, dma((2 * CHUNKS,)), dma((CHUNKS,)), dma, dma,
            dma((CHIPS,)), dma((CHIPS,)), dma((CHIPS,)), dma((CHIPS,)), dma((CHIPS,)), dma((CHIPS,)),
            dma((CHIPS,)), dma((CHIPS,)), dma, dma, dma((CHIPS,)), dma((CHIPS,)), dma((4,)), dma,
            pltpu.SemaphoreType.REGULAR((3,)),
        ],
        compiler_params=pltpu.CompilerParams(
            collective_id=0, has_side_effects=True, vmem_limit_bytes=24 << 20
        ),
    )(snapshots)
    kept, panel2, total, packed = [
        pltpu.with_memory_space_constraint(a, pltpu.VMEM) for a in (kept, panel2, total, packed)
    ]
    return pl.pallas_call(
        apply_kernel,
        name="apply",
        out_shape=[
            jax.ShapeDtypeStruct((PANEL, PANEL), F32),
            jax.ShapeDtypeStruct((PANEL, COLS), F32),
            jax.ShapeDtypeStruct((ROWS, COLS), F32),
        ],
        in_specs=[pl.BlockSpec(memory_space=pltpu.VMEM)] * 4,
        out_specs=[
            pl.BlockSpec(memory_space=pltpu.VMEM),
            pl.BlockSpec(memory_space=pltpu.VMEM),
            pl.BlockSpec(memory_space=pl.ANY),
        ],
        scratch_shapes=[
            pltpu.VMEM((ROWS, COLS), F32),
            pltpu.VMEM((3 * PANEL, COLS), BF16),
            dma((BLOCKS * COLS // TILE,)),
        ],
        compiler_params=pltpu.CompilerParams(vmem_limit_bytes=24 << 20),
    )(kept, panel2, total, packed)


def solution(mesh):
    in_specs = (P("rows", "cols"),)
    out_specs = (P(), P(None, "cols"), P("rows", "cols"))
    return jax.shard_map(body, mesh=mesh, in_specs=in_specs, out_specs=out_specs, check_vma=False)
```

```python
import jax
import jax.numpy as jnp
from jax import lax
from jax.experimental import pallas as pl
from jax.experimental.pallas import tpu as pltpu
from jax.sharding import PartitionSpec as P

MESH = pl.DeviceIdType.MESH
F32 = jnp.float32
BF16 = jnp.bfloat16
PANEL = 128
ROWS = 2048
COLS = 1024
HALF = COLS // 2
CHIPS = 16
BLOCK = 256
BLOCKS = ROWS // BLOCK
CHUNK = 64
CHUNKS = ROWS // CHUNK
RIGHT = 16
LEFT = CHUNKS - RIGHT
HEAD = RIGHT - LEFT
RIGHT_DIRECT = 6
LEFT_DIRECT = 8
PER = BLOCK // CHUNK
PIECE = PANEL // CHIPS
TILE = 512
GROUP = 16
SIZE = 4
UNIT = 128
UNITS = ROWS // UNIT
NEAR = sorted(
    ((dz, dy) for dz in range(SIZE) for dy in range(SIZE) if dz or dy),
    key=lambda at: min(at[0], SIZE - at[0]) + min(at[1], SIZE - at[1]),
)
FAR = NEAR[::-1]


def slot(at):
    return at[0] * SIZE + at[1]


def split(value):
    high = value.astype(BF16)
    low = (value - high.astype(F32)).astype(BF16)
    return high, low


def cross(left, right):
    return lax.dot_general(left, right, (((0,), (0,)), ((), ())), preferred_element_type=F32)


def plain(left, right):
    return lax.dot_general(left, right, (((1,), (0,)), ((), ())), preferred_element_type=F32)


def inverse(value):
    guess = pl.reciprocal(value, approx=True)
    return guess * (2.0 - value * guess)


def triple(value):
    one = value.astype(BF16)
    rest = value - one.astype(F32)
    two = rest.astype(BF16)
    return one, two, (rest - two.astype(F32)).astype(BF16)


def six_left(value):
    one, two, three = triple(value)
    return jnp.concatenate([one, one, two, two, one, three], axis=1)


def six_right(value):
    one, two, three = triple(value)
    return jnp.concatenate([one, two, one, two, three, one], axis=0)


def cholesky(gram_ref, packed_ref):
    shape = (GROUP, PANEL)
    sub = lax.broadcasted_iota(jnp.int32, shape, 0)
    lane = lax.broadcasted_iota(jnp.int32, shape, 1)

    def across(value, k):
        return jnp.broadcast_to(value[k : k + 1, :], shape)

    count = PANEL // GROUP
    lefts = [gram_ref[n * GROUP : (n + 1) * GROUP, :] for n in range(count)]
    rights = [(lane == sub + n * GROUP).astype(F32) for n in range(count)]
    for n in range(count):
        base = n * GROUP
        top, side = lefts[n], rights[n]
        columns = [jnp.broadcast_to(top[:, base + k : base + k + 1], shape) for k in range(GROUP)]
        pivot = across(columns[0], 0)
        pivots = pivot
        for k in range(GROUP - 1):
            recip = inverse(pivot)
            link = across(columns[k + 1], k)
            pivot = across(columns[k + 1], k + 1) - (link * recip) * link
            pivots = jnp.where(sub > k, pivot, pivots)
            factor = jnp.where(sub > k, columns[k] * recip, 0.0)
            for j in range(k + 1, GROUP):
                columns[j] = columns[j] - factor * across(columns[j], k)
            top, side = top - factor * across(top, k), side - factor * across(side, k)
        scale = lax.rsqrt(pivots)
        scale = scale * (1.5 - 0.5 * pivots * scale * scale)
        top = jnp.where(lane >= sub + base, top * scale, 0.0)
        side = side * scale
        packed_ref[base : base + GROUP, :] = jnp.where(lane >= sub + base, top, side)
        if n + 1 < count:
            one, two, three = triple(jnp.concatenate([top, side], axis=1))
            update = cross(
                jnp.concatenate([v[:, :PANEL] for v in (one, one, two, two, one, three)], axis=0),
                jnp.concatenate([one, two, one, two, three, one], axis=0),
            )
            for m in range(n + 1, count):
                rows = update[m * GROUP : (m + 1) * GROUP]
                lefts[m] = lefts[m] - rows[:, :PANEL]
                rights[m] = rights[m] - rows[:, PANEL:]


def gather_kernel(
    snap, kept, panel2, total, packed,
    pbuf, high, low, third, panel3, wacc, swap, mine, parts, gram, gparts, gsum, gswap, gfull,
    load_sem, pload_sem, bs_send, bs_recv, ex_send, ex_recv, rs_send, rs_recv, ag_send, ag_recv,
    fx_send, fx_recv, gr_send, gr_recv, gx_send, gx_recv, ga_send, ga_recv, u_send, u_recv, meet,
):
    row = lax.axis_index("rows")
    col = lax.axis_index("cols")
    chip = row // 2
    core = row % 2
    partner = (chip * 2 + 1 - core, col)
    high_axis, low_axis = chip // SIZE, chip % SIZE

    def away(at):
        return ((high_axis + at[0]) % SIZE) * SIZE + (low_axis + at[1]) % SIZE

    def peer(at):
        return away(at) * 2 + core

    along_x = [(row, (col + step) % SIZE) for step in (1, SIZE - 1)]
    along_low = [(peer((0, step)), col) for step in (1, SIZE - 1)]
    along_high = [(peer((step, 0)), col) for step in (1, SIZE - 1)]
    rounds = [along_x + along_low, along_high, along_high]

    def announce(index):
        for other in rounds[index]:
            pl.semaphore_signal(meet.at[index], inc=1, device_id=other, device_id_type=MESH)

    def await_round(index):
        pl.semaphore_wait(meet.at[index], len(rounds[index]))

    greeted = along_x + along_low + along_high + [partner]
    barrier = pltpu.get_barrier_semaphore()
    for other in greeted:
        pl.semaphore_signal(barrier, inc=1, device_id=other, device_id_type=MESH)

    def load(block):
        rows = pl.ds(pl.multiple_of(block * BLOCK, BLOCK), BLOCK)
        return pltpu.make_async_copy(snap.at[rows], kept.at[rows], load_sem.at[block])

    panel_load = pltpu.make_async_copy(snap.at[:, pl.ds(0, PANEL)], pbuf, pload_sem)

    @pl.when(col == 0)
    def _():
        panel_load.start()

    def start_load(block, carry):
        load(block).start()
        return carry

    @pl.when(col != 0)
    def _():
        lax.fori_loop(0, BLOCKS, start_load, 0)

    pl.semaphore_wait(barrier, len(greeted))

    def chunk_rows(chunk):
        return pl.ds(pl.multiple_of(chunk * CHUNK, CHUNK), CHUNK)

    def relay(chunk, target):
        rows = chunk_rows(chunk)
        return pltpu.make_async_remote_copy(
            src_ref=pbuf.at[rows], dst_ref=pbuf.at[rows], send_sem=bs_send.at[chunk],
            recv_sem=bs_recv.at[chunk], device_id=(row, target), device_id_type=MESH,
        )

    def first(chunk, target, extra=0):
        rows = chunk_rows(chunk)
        return pltpu.make_async_remote_copy(
            src_ref=pbuf.at[rows], dst_ref=pbuf.at[rows], send_sem=bs_send.at[chunk + extra],
            recv_sem=bs_recv.at[chunk], device_id=(row, target), device_id_type=MESH,
        )

    @pl.when(col == 0)
    def _():
        def send_right(step, carry):
            first(step, 1).start()
            return carry

        def send(step, carry):
            first(step + HEAD, 1).start()
            first(step + RIGHT, 3).start()
            return carry

        panel_load.wait()
        lax.fori_loop(0, HEAD, send_right, 0)
        lax.fori_loop(0, LEFT, send, 0)
        for step in range(max(RIGHT_DIRECT, LEFT_DIRECT)):
            if step < LEFT_DIRECT:
                first(CHUNKS - LEFT_DIRECT + step, 1, CHUNKS).start()
            if step < RIGHT_DIRECT:
                first(RIGHT - RIGHT_DIRECT + step, 3, CHUNKS).start()
        lax.fori_loop(0, BLOCKS, start_load, 0)
        announce(0)

    def block_rows(block):
        return pl.ds(pl.multiple_of(block * BLOCK, BLOCK), BLOCK)

    def widen(start, size):
        rows = pl.ds(pl.multiple_of(start, size), size)
        one, two, three = triple(pbuf[rows])
        panel2[rows, :PANEL] = one
        panel2[rows, PANEL:] = two
        panel3[rows] = three

    def prepare(block, carry):
        load(block).wait()
        rows = block_rows(block)
        high[rows], low[rows], third[rows] = triple(kept[rows])
        return carry

    def accumulate(start, size):
        rows = pl.ds(pl.multiple_of(start, size), size)
        both = panel2[rows]
        for n in range(COLS // 256):
            columns = pl.ds(n * 256, 256)
            one = cross(jnp.concatenate([both, panel3[rows]], axis=1), high[rows, columns])
            two = cross(both, low[rows, columns])
            three = cross(both[:, :PANEL], third[rows, columns])
            small = one[2 * PANEL :] + two[PANEL:] + three
            wacc[:, columns] += one[:PANEL] + (one[PANEL : 2 * PANEL] + two[:PANEL] + small)

    def gram_piece(step):
        other = away(step)
        return pltpu.make_async_remote_copy(
            src_ref=gram.at[pl.ds(pl.multiple_of(other * PIECE, PIECE), PIECE)], dst_ref=gparts.at[chip],
            send_sem=gr_send.at[slot(step)], recv_sem=gr_recv.at[chip], device_id=(peer(step), col), device_id_type=MESH,
        )

    def gram_arrived(step):
        other = away(step)
        return pltpu.make_async_remote_copy(
            src_ref=gram.at[pl.ds(0, PIECE)], dst_ref=gparts.at[other],
            send_sem=gr_send.at[slot(step)], recv_sem=gr_recv.at[other], device_id=(peer(step), col), device_id_type=MESH,
        )

    @pl.when(col == 0)
    def _():

        def one(block, carry):
            widen(block * BLOCK, BLOCK)
            return carry

        lax.fori_loop(0, BLOCKS, one, 0)
        full = cross(panel2[...], panel2[...])
        small = cross(panel2[:, :PANEL], panel3[...])
        small = small + small.T + full[PANEL:, PANEL:]
        gram[...] = full[:PANEL, :PANEL] + (full[:PANEL, PANEL:] + full[PANEL:, :PANEL] + small)

        await_round(0)
        announce(1)
        await_round(1)
        announce(2)
        await_round(2)
        for at in FAR:
            gram_piece(at).start()
        gparts[chip] = gram[pl.ds(pl.multiple_of(chip * PIECE, PIECE), PIECE)]

    wacc[...] = jnp.zeros_like(wacc)

    @pl.when(col == 0)
    def _():
        lax.fori_loop(0, BLOCKS, prepare, 0)

        def one(block, carry):
            accumulate(block * BLOCK, BLOCK)
            return carry

        lax.fori_loop(0, BLOCKS, one, 0)

    @pl.when(col != 0)
    def _():
        def ordered(step, right, head, count):
            turn = jnp.maximum(step - head, 0)
            both_ways = jnp.where(step < head, step, jnp.where(turn % 2 == 0, head, right) + turn // 2)
            straight = (step + jnp.where(col == 3, right, 0)) % count
            return jnp.where(col == 2, both_ways, straight)

        def pass_on(step):
            chunk = ordered(step, RIGHT, HEAD, CHUNKS)
            onward = jnp.where(chunk < RIGHT, col + 1, col - 1)
            shared = jnp.where(chunk < RIGHT, RIGHT - RIGHT_DIRECT, CHUNKS - LEFT_DIRECT)
            limit = jnp.where(col == 2, shared, CHUNKS)
            relay(chunk, 0).wait_recv()

            @pl.when((onward > 0) & (onward < 4) & (chunk < limit))
            def _():
                relay(chunk, onward).start()

        def work(index):
            unit = ordered(index, RIGHT // 2, HEAD // 2, UNITS)
            widen(unit * UNIT, UNIT)
            accumulate(unit * UNIT, UNIT)

        def early(step, carry):
            pass_on(step)
            prepare(step, 0)
            return carry

        def middle(step, carry):
            pass_on(step)
            work(step - BLOCKS)
            return carry

        def late(pair, carry):
            pass_on(2 * pair)
            work(pair - 1)
            pass_on(2 * pair + 1)
            return carry

        announce(0)

        lax.fori_loop(0, 2, early, 0)
        await_round(0)
        announce(1)
        lax.fori_loop(2, 4, early, 0)
        await_round(1)
        announce(2)
        lax.fori_loop(4, 6, early, 0)
        await_round(2)
        lax.fori_loop(6, BLOCKS, early, 0)
        lax.fori_loop(BLOCKS, 15, middle, 0)
        pass_on(15)
        lax.fori_loop(8, UNITS, late, 0)
        work(UNITS - 1)

    exchange = pltpu.make_async_remote_copy(
        src_ref=wacc.at[:, pl.ds(pl.multiple_of((1 - core) * HALF, HALF), HALF)], dst_ref=swap,
        send_sem=ex_send, recv_sem=ex_recv, device_id=partner, device_id_type=MESH,
    )
    exchange.start()

    gram_swap = pltpu.make_async_remote_copy(
        src_ref=gsum, dst_ref=gswap, send_sem=gx_send, recv_sem=gx_recv, device_id=partner, device_id_type=MESH,
    )

    def gram_gather(step):
        rows = pl.ds(pl.multiple_of(chip * PIECE, PIECE), PIECE)
        return pltpu.make_async_remote_copy(
            src_ref=gfull.at[rows], dst_ref=gfull.at[rows],
            send_sem=ga_send.at[slot(step)], recv_sem=ga_recv.at[chip], device_id=(peer(step), col), device_id_type=MESH,
        )

    def gram_gathered(step):
        other = away(step)
        rows = pl.ds(pl.multiple_of(other * PIECE, PIECE), PIECE)
        return pltpu.make_async_remote_copy(
            src_ref=gfull.at[rows], dst_ref=gfull.at[rows],
            send_sem=ga_send.at[slot(step)], recv_sem=ga_recv.at[other], device_id=(peer(step), col), device_id_type=MESH,
        )

    @pl.when(col == 0)
    def _():
        for at in NEAR:
            gram_arrived(at).wait_recv()
        gsum[...] = jnp.sum(gparts[...], axis=0)
        gram_swap.start()
        gram_swap.wait()
        gfull[pl.ds(pl.multiple_of(chip * PIECE, PIECE), PIECE)] = gsum[...] + gswap[...]

        for at in FAR:
            gram_gather(at).start()

    exchange.wait()
    mine[...] = wacc[:, pl.ds(pl.multiple_of(core * HALF, HALF), HALF)] + swap[...]

    def scatter(step):
        other = away(step)
        return pltpu.make_async_remote_copy(
            src_ref=mine.at[pl.ds(pl.multiple_of(other * PIECE, PIECE), PIECE)], dst_ref=parts.at[chip],
            send_sem=rs_send.at[slot(step)], recv_sem=rs_recv.at[chip], device_id=(peer(step), col), device_id_type=MESH,
        )

    def scattered(step):
        other = away(step)
        return pltpu.make_async_remote_copy(
            src_ref=mine.at[pl.ds(0, PIECE)], dst_ref=parts.at[other],
            send_sem=rs_send.at[slot(step)], recv_sem=rs_recv.at[other], device_id=(peer(step), col), device_id_type=MESH,
        )

    for at in FAR:
        scatter(at).start()
    parts[chip] = mine[pl.ds(pl.multiple_of(chip * PIECE, PIECE), PIECE)]

    def sent_on(chunk, carry):
        relay(chunk, 0).wait_send()
        return carry

    @pl.when(col == 1)
    def _():
        lax.fori_loop(0, RIGHT, sent_on, 0)

    @pl.when(col == 2)
    def _():
        lax.fori_loop(0, RIGHT - RIGHT_DIRECT, sent_on, 0)
        lax.fori_loop(RIGHT, CHUNKS - LEFT_DIRECT, sent_on, 0)

    @pl.when(col == 3)
    def _():
        lax.fori_loop(RIGHT, CHUNKS, sent_on, 0)

    def send_packed(target):
        return pltpu.make_async_remote_copy(
            src_ref=packed, dst_ref=packed, send_sem=u_send.at[target], recv_sem=u_recv,
            device_id=(row, target), device_id_type=MESH,
        )

    @pl.when(col == 0)
    def _():
        for at in NEAR:
            gram_gathered(at).wait_recv()
        cholesky(gfull, packed)
        for target in (2, 1, 3):
            send_packed(target).start()

        def sent(chunk, carry):
            first(chunk, 1).wait_send()
            return carry

        lax.fori_loop(0, CHUNKS, sent, 0)

        for step in range(LEFT_DIRECT):
            first(CHUNKS - LEFT_DIRECT + step, 1, CHUNKS).wait_send()
        for step in range(RIGHT_DIRECT):
            first(RIGHT - RIGHT_DIRECT + step, 3, CHUNKS).wait_send()

    for at in NEAR:
        scattered(at).wait_recv()
    half = pl.ds(pl.multiple_of(core * HALF, HALF), HALF)
    own = pl.ds(pl.multiple_of(chip * PIECE, PIECE), PIECE)
    total[own, half] = jnp.sum(parts[...], axis=0)

    def gather(step):
        return pltpu.make_async_remote_copy(
            src_ref=total.at[own, half], dst_ref=total.at[own, half],
            send_sem=ag_send.at[slot(step)], recv_sem=ag_recv.at[chip], device_id=(peer(step), col), device_id_type=MESH,
        )

    def gathered(step):
        other = away(step)
        rows = pl.ds(pl.multiple_of(other * PIECE, PIECE), PIECE)
        return pltpu.make_async_remote_copy(
            src_ref=total.at[rows, half], dst_ref=total.at[rows, half],
            send_sem=ag_send.at[slot(step)], recv_sem=ag_recv.at[other], device_id=(peer(step), col), device_id_type=MESH,
        )

    def onward(owner, columns):
        rows = pl.ds(pl.multiple_of(owner * PIECE, PIECE), PIECE)
        return pltpu.make_async_remote_copy(
            src_ref=total.at[rows, columns], dst_ref=total.at[rows, columns], send_sem=fx_send.at[owner],
            recv_sem=fx_recv.at[owner], device_id=partner, device_id_type=MESH,
        )

    for at in FAR:
        gather(at).start()
    onward(chip, half).start()
    for at in NEAR:
        scatter(at).wait_send()
    for at in NEAR:
        gathered(at).wait_recv()
        onward(away(at), half).start()
    other_half = pl.ds(pl.multiple_of((1 - core) * HALF, HALF), HALF)

    for at in NEAR:
        gather(at).wait_send()

    @pl.when(col == 0)
    def _():
        for at in NEAR:
            gram_piece(at).wait_send()
            gram_gather(at).wait_send()
        for target in (2, 1, 3):
            send_packed(target).wait_send()

    @pl.when(col != 0)
    def _():
        send_packed(0).wait_recv()

    def finish(owner, carry):
        onward(owner, half).wait_send()
        onward(owner, other_half).wait_recv()
        return carry

    lax.fori_loop(0, CHIPS, finish, 0)


def apply_kernel(kept, panel2, total, packed, factor, coupling, updated, out, x2, sems):
    both = packed[...]
    sub = lax.broadcasted_iota(jnp.int32, (PANEL, PANEL), 0)
    lane = lax.broadcasted_iota(jnp.int32, (PANEL, PANEL), 1)
    factor[...] = jnp.where(lane >= sub, both, 0.0) * (1.0 / 256.0)
    lower = jnp.where(lane < sub, both, jnp.where(lane == sub, 1.0 / both, 0.0))
    to_coupling, to_weights = six_left(lower), six_left(lower.T)
    copies = []
    for n in range(COLS // TILE):
        columns = pl.ds(n * TILE, TILE)
        c = plain(to_coupling, six_right(total[:, columns]))
        coupling[:, columns] = c
        xh, xl = split(plain(to_weights, six_right(c)))
        x2[:, columns] = jnp.concatenate([xh, xh, xl], axis=0)
        for block in range(BLOCKS):
            rows = pl.ds(block * BLOCK, BLOCK)
            p = panel2[rows]
            left = jnp.concatenate([p, p[:, :PANEL]], axis=1)
            out[rows, columns] = kept[rows, columns] - plain(left, x2[:, columns])
            copy = pltpu.make_async_copy(
                out.at[rows, columns], updated.at[rows, columns], sems.at[n * BLOCKS + block]
            )
            copy.start()
            copies.append(copy)
    for copy in copies:
        copy.wait()


def body(snapshots):
    dma = pltpu.SemaphoreType.DMA
    snapshots = pltpu.with_memory_space_constraint(snapshots, pltpu.HBM)
    kept, panel2, total, packed = pl.pallas_call(
        gather_kernel,
        name="panel_sums",
        out_shape=[
            pltpu.VMEM((ROWS, COLS), F32),
            pltpu.VMEM((ROWS, 2 * PANEL), BF16),
            pltpu.VMEM((PANEL, COLS), F32),
            pltpu.VMEM((PANEL, PANEL), F32),
        ],
        in_specs=[pl.BlockSpec(memory_space=pltpu.HBM)],
        out_specs=[pl.BlockSpec(memory_space=pltpu.VMEM)] * 4,
        scratch_shapes=[
            pltpu.VMEM((ROWS, PANEL), F32),
            pltpu.VMEM((ROWS, COLS), BF16),
            pltpu.VMEM((ROWS, COLS), BF16),
            pltpu.VMEM((ROWS, COLS), BF16),
            pltpu.VMEM((ROWS, PANEL), BF16),
            pltpu.VMEM((PANEL, COLS), F32),
            pltpu.VMEM((PANEL, HALF), F32),
            pltpu.VMEM((PANEL, HALF), F32),
            pltpu.VMEM((CHIPS, PIECE, HALF), F32),
            pltpu.VMEM((PANEL, PANEL), F32),
            pltpu.VMEM((CHIPS, PIECE, PANEL), F32),
            pltpu.VMEM((PIECE, PANEL), F32),
            pltpu.VMEM((PIECE, PANEL), F32),
            pltpu.VMEM((PANEL, PANEL), F32),
            dma((BLOCKS,)), dma, dma((2 * CHUNKS,)), dma((CHUNKS,)), dma, dma,
            dma((CHIPS,)), dma((CHIPS,)), dma((CHIPS,)), dma((CHIPS,)), dma((CHIPS,)), dma((CHIPS,)),
            dma((CHIPS,)), dma((CHIPS,)), dma, dma, dma((CHIPS,)), dma((CHIPS,)), dma((4,)), dma,
            pltpu.SemaphoreType.REGULAR((3,)),
        ],
        compiler_params=pltpu.CompilerParams(
            collective_id=0, has_side_effects=True, vmem_limit_bytes=30 << 20
        ),
    )(snapshots)
    kept, panel2, total, packed = [
        pltpu.with_memory_space_constraint(a, pltpu.VMEM) for a in (kept, panel2, total, packed)
    ]
    return pl.pallas_call(
        apply_kernel,
        name="apply",
        out_shape=[
            jax.ShapeDtypeStruct((PANEL, PANEL), F32),
            jax.ShapeDtypeStruct((PANEL, COLS), F32),
            jax.ShapeDtypeStruct((ROWS, COLS), F32),
        ],
        in_specs=[pl.BlockSpec(memory_space=pltpu.VMEM)] * 4,
        out_specs=[
            pl.BlockSpec(memory_space=pltpu.VMEM),
            pl.BlockSpec(memory_space=pltpu.VMEM),
            pl.BlockSpec(memory_space=pl.ANY),
        ],
        scratch_shapes=[
            pltpu.VMEM((ROWS, COLS), F32),
            pltpu.VMEM((3 * PANEL, COLS), BF16),
            dma((BLOCKS * COLS // TILE,)),
        ],
        compiler_params=pltpu.CompilerParams(vmem_limit_bytes=24 << 20),
    )(kept, panel2, total, packed)


def solution(mesh):
    in_specs = (P("rows", "cols"),)
    out_specs = (P(), P(None, "cols"), P("rows", "cols"))
    return jax.shard_map(body, mesh=mesh, in_specs=in_specs, out_specs=out_specs, check_vma=False)
```

```python
import jax
import jax.numpy as jnp
from jax import lax
from jax.experimental import pallas as pl
from jax.experimental.pallas import tpu as pltpu
from jax.sharding import PartitionSpec as P

MESH = pl.DeviceIdType.MESH
F32 = jnp.float32
BF16 = jnp.bfloat16
PANEL = 128
ROWS = 2048
COLS = 1024
HALF = COLS // 2
CHIPS = 16
BLOCK = 256
BLOCKS = ROWS // BLOCK
CHUNK = 64
CHUNKS = ROWS // CHUNK
RIGHT = 16
LEFT = CHUNKS - RIGHT
HEAD = RIGHT - LEFT
RIGHT_DIRECT = 6
LEFT_DIRECT = 8
PER = BLOCK // CHUNK
PIECE = PANEL // CHIPS
TILE = 512
GROUP = 16
SIZE = 4
UNIT = 128
UNITS = ROWS // UNIT
NEAR = sorted(
    ((dz, dy) for dz in range(SIZE) for dy in range(SIZE) if dz or dy),
    key=lambda at: min(at[0], SIZE - at[0]) + min(at[1], SIZE - at[1]),
)
FAR = NEAR[::-1]


def slot(at):
    return at[0] * SIZE + at[1]


def split(value):
    high = value.astype(BF16)
    low = (value - high.astype(F32)).astype(BF16)
    return high, low


def cross(left, right):
    return lax.dot_general(left, right, (((0,), (0,)), ((), ())), preferred_element_type=F32)


def plain(left, right):
    return lax.dot_general(left, right, (((1,), (0,)), ((), ())), preferred_element_type=F32)


def inverse(value):
    guess = pl.reciprocal(value, approx=True)
    return guess * (2.0 - value * guess)


def triple(value):
    one = value.astype(BF16)
    rest = value - one.astype(F32)
    two = rest.astype(BF16)
    return one, two, (rest - two.astype(F32)).astype(BF16)


def six_left(value):
    one, two, three = triple(value)
    return jnp.concatenate([one, one, two, two, one, three], axis=1)


def six_right(value):
    one, two, three = triple(value)
    return jnp.concatenate([one, two, one, two, three, one], axis=0)


def cholesky(gram_ref, packed_ref):
    shape = (GROUP, PANEL)
    sub = lax.broadcasted_iota(jnp.int32, shape, 0)
    lane = lax.broadcasted_iota(jnp.int32, shape, 1)

    def across(value, k):
        return jnp.broadcast_to(value[k : k + 1, :], shape)

    count = PANEL // GROUP
    lefts = [gram_ref[n * GROUP : (n + 1) * GROUP, :] for n in range(count)]
    rights = [(lane == sub + n * GROUP).astype(F32) for n in range(count)]
    for n in range(count):
        base = n * GROUP
        top, side = lefts[n], rights[n]
        columns = [jnp.broadcast_to(top[:, base + k : base + k + 1], shape) for k in range(GROUP)]
        pivot = across(columns[0], 0)
        pivots = pivot
        for k in range(GROUP - 1):
            recip = inverse(pivot)
            link = across(columns[k + 1], k)
            pivot = across(columns[k + 1], k + 1) - (link * recip) * link
            pivots = jnp.where(sub > k, pivot, pivots)
            factor = jnp.where(sub > k, columns[k] * recip, 0.0)
            for j in range(k + 1, GROUP):
                columns[j] = columns[j] - factor * across(columns[j], k)
            top, side = top - factor * across(top, k), side - factor * across(side, k)
        scale = lax.rsqrt(pivots)
        scale = scale * (1.5 - 0.5 * pivots * scale * scale)
        top = jnp.where(lane >= sub + base, top * scale, 0.0)
        side = side * scale
        packed_ref[base : base + GROUP, :] = jnp.where(lane >= sub + base, top, side)
        if n + 1 < count:
            one, two, three = triple(jnp.concatenate([top, side], axis=1))
            update = cross(
                jnp.concatenate([v[:, :PANEL] for v in (one, one, two, two, one, three)], axis=0),
                jnp.concatenate([one, two, one, two, three, one], axis=0),
            )
            for m in range(n + 1, count):
                rows = update[m * GROUP : (m + 1) * GROUP]
                lefts[m] = lefts[m] - rows[:, :PANEL]
                rights[m] = rights[m] - rows[:, PANEL:]


def gather_kernel(
    snap, kept, panel2, total, packed,
    pbuf, high, low, third, panel3, wacc, swap, mine, parts, gram, gparts, gsum, gswap, gfull,
    load_sem, pload_sem, bs_send, bs_recv, ex_send, ex_recv, rs_send, rs_recv, ag_send, ag_recv,
    fx_send, fx_recv, gr_send, gr_recv, gx_send, gx_recv, ga_send, ga_recv, u_send, u_recv, meet,
):
    row = lax.axis_index("rows")
    col = lax.axis_index("cols")
    chip = row // 2
    core = row % 2
    partner = (chip * 2 + 1 - core, col)
    high_axis, low_axis = chip // SIZE, chip % SIZE

    def away(at):
        return ((high_axis + at[0]) % SIZE) * SIZE + (low_axis + at[1]) % SIZE

    def peer(at):
        return away(at) * 2 + core

    along_x = [(row, (col + step) % SIZE) for step in (1, SIZE - 1)]
    along_low = [(peer((0, step)), col) for step in (1, SIZE - 1)]
    along_high = [(peer((step, 0)), col) for step in (1, SIZE - 1)]
    rounds = [along_x + along_low, along_high, along_high]

    def announce(index):
        for other in rounds[index]:
            pl.semaphore_signal(meet.at[index], inc=1, device_id=other, device_id_type=MESH)

    def await_round(index):
        pl.semaphore_wait(meet.at[index], len(rounds[index]))

    greeted = along_x + along_low + along_high + [partner]
    barrier = pltpu.get_barrier_semaphore()
    for other in greeted:
        pl.semaphore_signal(barrier, inc=1, device_id=other, device_id_type=MESH)

    def load(block):
        rows = pl.ds(pl.multiple_of(block * BLOCK, BLOCK), BLOCK)
        return pltpu.make_async_copy(snap.at[rows], kept.at[rows], load_sem.at[block])

    panel_load = pltpu.make_async_copy(snap.at[:, pl.ds(0, PANEL)], pbuf, pload_sem)

    @pl.when(col == 0)
    def _():
        panel_load.start()

    def start_load(block, carry):
        load(block).start()
        return carry

    @pl.when(col != 0)
    def _():
        lax.fori_loop(0, BLOCKS, start_load, 0)

    pl.semaphore_wait(barrier, len(greeted))

    def chunk_rows(chunk):
        return pl.ds(pl.multiple_of(chunk * CHUNK, CHUNK), CHUNK)

    def relay(chunk, target):
        rows = chunk_rows(chunk)
        return pltpu.make_async_remote_copy(
            src_ref=pbuf.at[rows], dst_ref=pbuf.at[rows], send_sem=bs_send.at[chunk],
            recv_sem=bs_recv.at[chunk], device_id=(row, target), device_id_type=MESH,
        )

    def first(chunk, target, extra=0):
        rows = chunk_rows(chunk)
        return pltpu.make_async_remote_copy(
            src_ref=pbuf.at[rows], dst_ref=pbuf.at[rows], send_sem=bs_send.at[chunk + extra],
            recv_sem=bs_recv.at[chunk], device_id=(row, target), device_id_type=MESH,
        )

    @pl.when(col == 0)
    def _():
        def send_right(step, carry):
            first(step, 1).start()
            return carry

        def send(step, carry):
            first(step + HEAD, 1).start()
            first(step + RIGHT, 3).start()
            return carry

        panel_load.wait()
        lax.fori_loop(0, HEAD, send_right, 0)
        lax.fori_loop(0, LEFT, send, 0)
        for step in range(max(RIGHT_DIRECT, LEFT_DIRECT)):
            if step < LEFT_DIRECT:
                first(CHUNKS - LEFT_DIRECT + step, 1, CHUNKS).start()
            if step < RIGHT_DIRECT:
                first(RIGHT - RIGHT_DIRECT + step, 3, CHUNKS).start()
        lax.fori_loop(0, BLOCKS, start_load, 0)
        announce(0)

    def block_rows(block):
        return pl.ds(pl.multiple_of(block * BLOCK, BLOCK), BLOCK)

    def widen(start, size):
        rows = pl.ds(pl.multiple_of(start, size), size)
        one, two, three = triple(pbuf[rows])
        panel2[rows, :PANEL] = one
        panel2[rows, PANEL:] = two
        panel3[rows] = three

    def prepare(block, carry):
        load(block).wait()
        rows = block_rows(block)
        high[rows], low[rows], third[rows] = triple(kept[rows])
        return carry

    def accumulate(start, size):
        rows = pl.ds(pl.multiple_of(start, size), size)
        turned = jnp.concatenate([panel2[rows], panel3[rows]], axis=1).T
        for n in range(COLS // 256):
            columns = pl.ds(n * 256, 256)
            one = plain(turned, high[rows, columns])
            two = plain(turned[: 2 * PANEL], low[rows, columns])
            three = plain(turned[:PANEL], third[rows, columns])
            small = one[2 * PANEL :] + two[PANEL:] + three
            wacc[:, columns] += one[:PANEL] + (one[PANEL : 2 * PANEL] + two[:PANEL] + small)

    def gram_piece(step):
        other = away(step)
        return pltpu.make_async_remote_copy(
            src_ref=gram.at[pl.ds(pl.multiple_of(other * PIECE, PIECE), PIECE)], dst_ref=gparts.at[chip],
            send_sem=gr_send.at[slot(step)], recv_sem=gr_recv.at[chip], device_id=(peer(step), col), device_id_type=MESH,
        )

    def gram_arrived(step):
        other = away(step)
        return pltpu.make_async_remote_copy(
            src_ref=gram.at[pl.ds(0, PIECE)], dst_ref=gparts.at[other],
            send_sem=gr_send.at[slot(step)], recv_sem=gr_recv.at[other], device_id=(peer(step), col), device_id_type=MESH,
        )

    @pl.when(col == 0)
    def _():

        def one(block, carry):
            widen(block * BLOCK, BLOCK)
            return carry

        lax.fori_loop(0, BLOCKS, one, 0)
        full = cross(panel2[...], panel2[...])
        small = cross(panel2[:, :PANEL], panel3[...])
        small = small + small.T + full[PANEL:, PANEL:]
        gram[...] = full[:PANEL, :PANEL] + (full[:PANEL, PANEL:] + full[PANEL:, :PANEL] + small)

        await_round(0)
        announce(1)
        await_round(1)
        announce(2)
        await_round(2)
        for at in FAR:
            gram_piece(at).start()
        gparts[chip] = gram[pl.ds(pl.multiple_of(chip * PIECE, PIECE), PIECE)]

    wacc[...] = jnp.zeros_like(wacc)

    @pl.when(col == 0)
    def _():
        lax.fori_loop(0, BLOCKS, prepare, 0)

        def one(block, carry):
            accumulate(block * BLOCK, BLOCK)
            return carry

        lax.fori_loop(0, BLOCKS, one, 0)

    @pl.when(col != 0)
    def _():
        def ordered(step, right, head, count):
            turn = jnp.maximum(step - head, 0)
            both_ways = jnp.where(step < head, step, jnp.where(turn % 2 == 0, head, right) + turn // 2)
            straight = (step + jnp.where(col == 3, right, 0)) % count
            return jnp.where(col == 2, both_ways, straight)

        def pass_on(step):
            chunk = ordered(step, RIGHT, HEAD, CHUNKS)
            onward = jnp.where(chunk < RIGHT, col + 1, col - 1)
            shared = jnp.where(chunk < RIGHT, RIGHT - RIGHT_DIRECT, CHUNKS - LEFT_DIRECT)
            limit = jnp.where(col == 2, shared, CHUNKS)
            relay(chunk, 0).wait_recv()

            @pl.when((onward > 0) & (onward < 4) & (chunk < limit))
            def _():
                relay(chunk, onward).start()

        def work(index):
            unit = ordered(index, RIGHT // 2, HEAD // 2, UNITS)
            widen(unit * UNIT, UNIT)
            accumulate(unit * UNIT, UNIT)

        def early(step, carry):
            pass_on(step)
            prepare(step, 0)
            return carry

        def middle(step, carry):
            pass_on(step)
            work(step - BLOCKS)
            return carry

        def late(pair, carry):
            pass_on(2 * pair)
            work(pair - 1)
            pass_on(2 * pair + 1)
            return carry

        announce(0)

        lax.fori_loop(0, 2, early, 0)
        await_round(0)
        announce(1)
        lax.fori_loop(2, 4, early, 0)
        await_round(1)
        announce(2)
        lax.fori_loop(4, 6, early, 0)
        await_round(2)
        lax.fori_loop(6, BLOCKS, early, 0)
        lax.fori_loop(BLOCKS, 15, middle, 0)
        pass_on(15)
        lax.fori_loop(8, UNITS, late, 0)
        work(UNITS - 1)

    exchange = pltpu.make_async_remote_copy(
        src_ref=wacc.at[:, pl.ds(pl.multiple_of((1 - core) * HALF, HALF), HALF)], dst_ref=swap,
        send_sem=ex_send, recv_sem=ex_recv, device_id=partner, device_id_type=MESH,
    )
    exchange.start()

    gram_swap = pltpu.make_async_remote_copy(
        src_ref=gsum, dst_ref=gswap, send_sem=gx_send, recv_sem=gx_recv, device_id=partner, device_id_type=MESH,
    )

    def gram_gather(step):
        rows = pl.ds(pl.multiple_of(chip * PIECE, PIECE), PIECE)
        return pltpu.make_async_remote_copy(
            src_ref=gfull.at[rows], dst_ref=gfull.at[rows],
            send_sem=ga_send.at[slot(step)], recv_sem=ga_recv.at[chip], device_id=(peer(step), col), device_id_type=MESH,
        )

    def gram_gathered(step):
        other = away(step)
        rows = pl.ds(pl.multiple_of(other * PIECE, PIECE), PIECE)
        return pltpu.make_async_remote_copy(
            src_ref=gfull.at[rows], dst_ref=gfull.at[rows],
            send_sem=ga_send.at[slot(step)], recv_sem=ga_recv.at[other], device_id=(peer(step), col), device_id_type=MESH,
        )

    @pl.when(col == 0)
    def _():
        for at in NEAR:
            gram_arrived(at).wait_recv()
        gsum[...] = jnp.sum(gparts[...], axis=0)
        gram_swap.start()
        gram_swap.wait()
        gfull[pl.ds(pl.multiple_of(chip * PIECE, PIECE), PIECE)] = gsum[...] + gswap[...]

        for at in FAR:
            gram_gather(at).start()

    exchange.wait()
    mine[...] = wacc[:, pl.ds(pl.multiple_of(core * HALF, HALF), HALF)] + swap[...]

    def scatter(step):
        other = away(step)
        return pltpu.make_async_remote_copy(
            src_ref=mine.at[pl.ds(pl.multiple_of(other * PIECE, PIECE), PIECE)], dst_ref=parts.at[chip],
            send_sem=rs_send.at[slot(step)], recv_sem=rs_recv.at[chip], device_id=(peer(step), col), device_id_type=MESH,
        )

    def scattered(step):
        other = away(step)
        return pltpu.make_async_remote_copy(
            src_ref=mine.at[pl.ds(0, PIECE)], dst_ref=parts.at[other],
            send_sem=rs_send.at[slot(step)], recv_sem=rs_recv.at[other], device_id=(peer(step), col), device_id_type=MESH,
        )

    for at in FAR:
        scatter(at).start()
    parts[chip] = mine[pl.ds(pl.multiple_of(chip * PIECE, PIECE), PIECE)]

    def sent_on(chunk, carry):
        relay(chunk, 0).wait_send()
        return carry

    @pl.when(col == 1)
    def _():
        lax.fori_loop(0, RIGHT, sent_on, 0)

    @pl.when(col == 2)
    def _():
        lax.fori_loop(0, RIGHT - RIGHT_DIRECT, sent_on, 0)
        lax.fori_loop(RIGHT, CHUNKS - LEFT_DIRECT, sent_on, 0)

    @pl.when(col == 3)
    def _():
        lax.fori_loop(RIGHT, CHUNKS, sent_on, 0)

    def send_packed(target):
        return pltpu.make_async_remote_copy(
            src_ref=packed, dst_ref=packed, send_sem=u_send.at[target], recv_sem=u_recv,
            device_id=(row, target), device_id_type=MESH,
        )

    @pl.when(col == 0)
    def _():
        for at in NEAR:
            gram_gathered(at).wait_recv()
        cholesky(gfull, packed)
        for target in (2, 1, 3):
            send_packed(target).start()

        def sent(chunk, carry):
            first(chunk, 1).wait_send()
            return carry

        lax.fori_loop(0, CHUNKS, sent, 0)

        for step in range(LEFT_DIRECT):
            first(CHUNKS - LEFT_DIRECT + step, 1, CHUNKS).wait_send()
        for step in range(RIGHT_DIRECT):
            first(RIGHT - RIGHT_DIRECT + step, 3, CHUNKS).wait_send()

    for at in NEAR:
        scattered(at).wait_recv()
    half = pl.ds(pl.multiple_of(core * HALF, HALF), HALF)
    own = pl.ds(pl.multiple_of(chip * PIECE, PIECE), PIECE)
    total[own, half] = jnp.sum(parts[...], axis=0)

    def gather(step):
        return pltpu.make_async_remote_copy(
            src_ref=total.at[own, half], dst_ref=total.at[own, half],
            send_sem=ag_send.at[slot(step)], recv_sem=ag_recv.at[chip], device_id=(peer(step), col), device_id_type=MESH,
        )

    def gathered(step):
        other = away(step)
        rows = pl.ds(pl.multiple_of(other * PIECE, PIECE), PIECE)
        return pltpu.make_async_remote_copy(
            src_ref=total.at[rows, half], dst_ref=total.at[rows, half],
            send_sem=ag_send.at[slot(step)], recv_sem=ag_recv.at[other], device_id=(peer(step), col), device_id_type=MESH,
        )

    def onward(owner, columns):
        rows = pl.ds(pl.multiple_of(owner * PIECE, PIECE), PIECE)
        return pltpu.make_async_remote_copy(
            src_ref=total.at[rows, columns], dst_ref=total.at[rows, columns], send_sem=fx_send.at[owner],
            recv_sem=fx_recv.at[owner], device_id=partner, device_id_type=MESH,
        )

    for at in FAR:
        gather(at).start()
    onward(chip, half).start()
    for at in NEAR:
        scatter(at).wait_send()
    for at in NEAR:
        gathered(at).wait_recv()
        onward(away(at), half).start()
    other_half = pl.ds(pl.multiple_of((1 - core) * HALF, HALF), HALF)

    for at in NEAR:
        gather(at).wait_send()

    @pl.when(col == 0)
    def _():
        for at in NEAR:
            gram_piece(at).wait_send()
            gram_gather(at).wait_send()
        for target in (2, 1, 3):
            send_packed(target).wait_send()

    @pl.when(col != 0)
    def _():
        send_packed(0).wait_recv()

    def finish(owner, carry):
        onward(owner, half).wait_send()
        onward(owner, other_half).wait_recv()
        return carry

    lax.fori_loop(0, CHIPS, finish, 0)


def apply_kernel(kept, panel2, total, packed, factor, coupling, updated, out, x2, sems):
    both = packed[...]
    sub = lax.broadcasted_iota(jnp.int32, (PANEL, PANEL), 0)
    lane = lax.broadcasted_iota(jnp.int32, (PANEL, PANEL), 1)
    factor[...] = jnp.where(lane >= sub, both, 0.0) * (1.0 / 256.0)
    lower = jnp.where(lane < sub, both, jnp.where(lane == sub, 1.0 / both, 0.0))
    to_coupling, to_weights = six_left(lower), six_left(lower.T)
    copies = []
    for n in range(COLS // TILE):
        columns = pl.ds(n * TILE, TILE)
        c = plain(to_coupling, six_right(total[:, columns]))
        coupling[:, columns] = c
        xh, xl = split(plain(to_weights, six_right(c)))
        x2[:, columns] = jnp.concatenate([xh, xh, xl], axis=0)
        for block in range(BLOCKS):
            rows = pl.ds(block * BLOCK, BLOCK)
            p = panel2[rows]
            left = jnp.concatenate([p, p[:, :PANEL]], axis=1)
            out[rows, columns] = kept[rows, columns] - plain(left, x2[:, columns])
            copy = pltpu.make_async_copy(
                out.at[rows, columns], updated.at[rows, columns], sems.at[n * BLOCKS + block]
            )
            copy.start()
            copies.append(copy)
    for copy in copies:
        copy.wait()


def body(snapshots):
    dma = pltpu.SemaphoreType.DMA
    snapshots = pltpu.with_memory_space_constraint(snapshots, pltpu.HBM)
    kept, panel2, total, packed = pl.pallas_call(
        gather_kernel,
        name="panel_sums",
        out_shape=[
            pltpu.VMEM((ROWS, COLS), F32),
            pltpu.VMEM((ROWS, 2 * PANEL), BF16),
            pltpu.VMEM((PANEL, COLS), F32),
            pltpu.VMEM((PANEL, PANEL), F32),
        ],
        in_specs=[pl.BlockSpec(memory_space=pltpu.HBM)],
        out_specs=[pl.BlockSpec(memory_space=pltpu.VMEM)] * 4,
        scratch_shapes=[
            pltpu.VMEM((ROWS, PANEL), F32),
            pltpu.VMEM((ROWS, COLS), BF16),
            pltpu.VMEM((ROWS, COLS), BF16),
            pltpu.VMEM((ROWS, COLS), BF16),
            pltpu.VMEM((ROWS, PANEL), BF16),
            pltpu.VMEM((PANEL, COLS), F32),
            pltpu.VMEM((PANEL, HALF), F32),
            pltpu.VMEM((PANEL, HALF), F32),
            pltpu.VMEM((CHIPS, PIECE, HALF), F32),
            pltpu.VMEM((PANEL, PANEL), F32),
            pltpu.VMEM((CHIPS, PIECE, PANEL), F32),
            pltpu.VMEM((PIECE, PANEL), F32),
            pltpu.VMEM((PIECE, PANEL), F32),
            pltpu.VMEM((PANEL, PANEL), F32),
            dma((BLOCKS,)), dma, dma((2 * CHUNKS,)), dma((CHUNKS,)), dma, dma,
            dma((CHIPS,)), dma((CHIPS,)), dma((CHIPS,)), dma((CHIPS,)), dma((CHIPS,)), dma((CHIPS,)),
            dma((CHIPS,)), dma((CHIPS,)), dma, dma, dma((CHIPS,)), dma((CHIPS,)), dma((4,)), dma,
            pltpu.SemaphoreType.REGULAR((3,)),
        ],
        compiler_params=pltpu.CompilerParams(
            collective_id=0, has_side_effects=True, vmem_limit_bytes=30 << 20
        ),
    )(snapshots)
    kept, panel2, total, packed = [
        pltpu.with_memory_space_constraint(a, pltpu.VMEM) for a in (kept, panel2, total, packed)
    ]
    return pl.pallas_call(
        apply_kernel,
        name="apply",
        out_shape=[
            jax.ShapeDtypeStruct((PANEL, PANEL), F32),
            jax.ShapeDtypeStruct((PANEL, COLS), F32),
            jax.ShapeDtypeStruct((ROWS, COLS), F32),
        ],
        in_specs=[pl.BlockSpec(memory_space=pltpu.VMEM)] * 4,
        out_specs=[
            pl.BlockSpec(memory_space=pltpu.VMEM),
            pl.BlockSpec(memory_space=pltpu.VMEM),
            pl.BlockSpec(memory_space=pl.ANY),
        ],
        scratch_shapes=[
            pltpu.VMEM((ROWS, COLS), F32),
            pltpu.VMEM((3 * PANEL, COLS), BF16),
            dma((BLOCKS * COLS // TILE,)),
        ],
        compiler_params=pltpu.CompilerParams(vmem_limit_bytes=24 << 20),
    )(kept, panel2, total, packed)


def solution(mesh):
    in_specs = (P("rows", "cols"),)
    out_specs = (P(), P(None, "cols"), P("rows", "cols"))
    return jax.shard_map(body, mesh=mesh, in_specs=in_specs, out_specs=out_specs, check_vma=False)
```

```python
import jax
import jax.numpy as jnp
from jax import lax
from jax.experimental import pallas as pl
from jax.experimental.pallas import tpu as pltpu
from jax.sharding import PartitionSpec as P

MESH = pl.DeviceIdType.MESH
F32 = jnp.float32
BF16 = jnp.bfloat16
PANEL = 128
ROWS = 2048
COLS = 1024
HALF = COLS // 2
CHIPS = 16
BLOCK = 256
BLOCKS = ROWS // BLOCK
CHUNK = 64
CHUNKS = ROWS // CHUNK
RIGHT = 16
LEFT = CHUNKS - RIGHT
HEAD = RIGHT - LEFT
RIGHT_DIRECT = 6
LEFT_DIRECT = 8
PER = BLOCK // CHUNK
PIECE = PANEL // CHIPS
TILE = 512
GROUP = 16
SIZE = 4
UNIT = 128
UNITS = ROWS // UNIT
NEAR = sorted(
    ((dz, dy) for dz in range(SIZE) for dy in range(SIZE) if dz or dy),
    key=lambda at: min(at[0], SIZE - at[0]) + min(at[1], SIZE - at[1]),
)
FAR = NEAR[::-1]


def slot(at):
    return at[0] * SIZE + at[1]


def split(value):
    high = value.astype(BF16)
    low = (value - high.astype(F32)).astype(BF16)
    return high, low


def cross(left, right):
    return lax.dot_general(left, right, (((0,), (0,)), ((), ())), preferred_element_type=F32)


def plain(left, right):
    return lax.dot_general(left, right, (((1,), (0,)), ((), ())), preferred_element_type=F32)


def inverse(value):
    guess = pl.reciprocal(value, approx=True)
    return guess * (2.0 - value * guess)


def triple(value):
    one = value.astype(BF16)
    rest = value - one.astype(F32)
    two = rest.astype(BF16)
    return one, two, (rest - two.astype(F32)).astype(BF16)


def six_left(value):
    one, two, three = triple(value)
    return jnp.concatenate([one, one, two, two, one, three], axis=1)


def six_right(value):
    one, two, three = triple(value)
    return jnp.concatenate([one, two, one, two, three, one], axis=0)


def cholesky(gram_ref, packed_ref):
    shape = (GROUP, PANEL)
    sub = lax.broadcasted_iota(jnp.int32, shape, 0)
    lane = lax.broadcasted_iota(jnp.int32, shape, 1)

    def across(value, k):
        return jnp.broadcast_to(value[k : k + 1, :], shape)

    count = PANEL // GROUP
    lefts = [gram_ref[n * GROUP : (n + 1) * GROUP, :] for n in range(count)]
    rights = [(lane == sub + n * GROUP).astype(F32) for n in range(count)]
    for n in range(count):
        base = n * GROUP
        top, side = lefts[n], rights[n]
        columns = [jnp.broadcast_to(top[:, base + k : base + k + 1], shape) for k in range(GROUP)]
        pivot = across(columns[0], 0)
        pivots = pivot
        for k in range(GROUP - 1):
            recip = inverse(pivot)
            link = across(columns[k + 1], k)
            pivot = across(columns[k + 1], k + 1) - (link * recip) * link
            pivots = jnp.where(sub > k, pivot, pivots)
            factor = jnp.where(sub > k, columns[k] * recip, 0.0)
            for j in range(k + 1, GROUP):
                columns[j] = columns[j] - factor * across(columns[j], k)
            top, side = top - factor * across(top, k), side - factor * across(side, k)
        scale = lax.rsqrt(pivots)
        scale = scale * (1.5 - 0.5 * pivots * scale * scale)
        top = jnp.where(lane >= sub + base, top * scale, 0.0)
        side = side * scale
        packed_ref[base : base + GROUP, :] = jnp.where(lane >= sub + base, top, side)
        if n + 1 < count:
            one, two, three = triple(jnp.concatenate([top, side], axis=1))
            update = cross(
                jnp.concatenate([v[:, :PANEL] for v in (one, one, two, two, one, three)], axis=0),
                jnp.concatenate([one, two, one, two, three, one], axis=0),
            )
            for m in range(n + 1, count):
                rows = update[m * GROUP : (m + 1) * GROUP]
                lefts[m] = lefts[m] - rows[:, :PANEL]
                rights[m] = rights[m] - rows[:, PANEL:]


def gather_kernel(
    snap, kept, panel2, total, packed,
    pbuf, high, low, third, panel3, wacc, swap, mine, parts, gram, gparts, gsum, gswap, gfull,
    load_sem, pload_sem, bs_send, bs_recv, ex_send, ex_recv, rs_send, rs_recv, ag_send, ag_recv,
    fx_send, fx_recv, gr_send, gr_recv, gx_send, gx_recv, ga_send, ga_recv, u_send, u_recv, meet,
):
    row = lax.axis_index("rows")
    col = lax.axis_index("cols")
    chip = row // 2
    core = row % 2
    partner = (chip * 2 + 1 - core, col)
    high_axis, low_axis = chip // SIZE, chip % SIZE

    def away(at):
        return ((high_axis + at[0]) % SIZE) * SIZE + (low_axis + at[1]) % SIZE

    def peer(at):
        return away(at) * 2 + core

    along_x = [(row, (col + step) % SIZE) for step in (1, SIZE - 1)]
    along_low = [(peer((0, step)), col) for step in (1, SIZE - 1)]
    along_high = [(peer((step, 0)), col) for step in (1, SIZE - 1)]
    rounds = [along_x + along_low, along_high, along_high]

    def announce(index):
        for other in rounds[index]:
            pl.semaphore_signal(meet.at[index], inc=1, device_id=other, device_id_type=MESH)

    def await_round(index):
        pl.semaphore_wait(meet.at[index], len(rounds[index]))

    greeted = along_x + along_low + along_high + [partner]
    barrier = pltpu.get_barrier_semaphore()
    for other in greeted:
        pl.semaphore_signal(barrier, inc=1, device_id=other, device_id_type=MESH)

    def load(block):
        rows = pl.ds(pl.multiple_of(block * BLOCK, BLOCK), BLOCK)
        return pltpu.make_async_copy(snap.at[rows], kept.at[rows], load_sem.at[block])

    panel_load = pltpu.make_async_copy(snap.at[:, pl.ds(0, PANEL)], pbuf, pload_sem)

    @pl.when(col == 0)
    def _():
        panel_load.start()

    def start_load(block, carry):
        load(block).start()
        return carry

    @pl.when(col != 0)
    def _():
        lax.fori_loop(0, BLOCKS, start_load, 0)

    pl.semaphore_wait(barrier, len(greeted))

    def chunk_rows(chunk):
        return pl.ds(pl.multiple_of(chunk * CHUNK, CHUNK), CHUNK)

    def relay(chunk, target):
        rows = chunk_rows(chunk)
        return pltpu.make_async_remote_copy(
            src_ref=pbuf.at[rows], dst_ref=pbuf.at[rows], send_sem=bs_send.at[chunk],
            recv_sem=bs_recv.at[chunk], device_id=(row, target), device_id_type=MESH,
        )

    def first(chunk, target, extra=0):
        rows = chunk_rows(chunk)
        return pltpu.make_async_remote_copy(
            src_ref=pbuf.at[rows], dst_ref=pbuf.at[rows], send_sem=bs_send.at[chunk + extra],
            recv_sem=bs_recv.at[chunk], device_id=(row, target), device_id_type=MESH,
        )

    @pl.when(col == 0)
    def _():
        def send_right(step, carry):
            first(step, 1).start()
            return carry

        def send(step, carry):
            first(step + HEAD, 1).start()
            first(step + RIGHT, 3).start()
            return carry

        panel_load.wait()
        lax.fori_loop(0, HEAD, send_right, 0)
        lax.fori_loop(0, LEFT, send, 0)
        for step in range(max(RIGHT_DIRECT, LEFT_DIRECT)):
            if step < LEFT_DIRECT:
                first(CHUNKS - LEFT_DIRECT + step, 1, CHUNKS).start()
            if step < RIGHT_DIRECT:
                first(RIGHT - RIGHT_DIRECT + step, 3, CHUNKS).start()
        lax.fori_loop(0, BLOCKS, start_load, 0)
        announce(0)

    def block_rows(block):
        return pl.ds(pl.multiple_of(block * BLOCK, BLOCK), BLOCK)

    def widen(start, size):
        rows = pl.ds(pl.multiple_of(start, size), size)
        one, two, three = triple(pbuf[rows])
        panel2[rows, :PANEL] = one
        panel2[rows, PANEL:] = two
        panel3[rows] = three

    def prepare(block, carry):
        load(block).wait()
        rows = block_rows(block)
        high[rows], low[rows], third[rows] = triple(kept[rows])
        return carry

    def accumulate(start, size):
        rows = pl.ds(pl.multiple_of(start, size), size)
        turned = jnp.concatenate([panel2[rows], panel3[rows]], axis=1).T
        for n in range(COLS // 256):
            columns = pl.ds(n * 256, 256)
            one = plain(turned, high[rows, columns])
            two = plain(turned[: 2 * PANEL], low[rows, columns])
            three = plain(turned[:PANEL], third[rows, columns])
            small = one[2 * PANEL :] + two[PANEL:] + three
            wacc[:, columns] += one[:PANEL] + (one[PANEL : 2 * PANEL] + two[:PANEL] + small)

    def gram_piece(step):
        other = away(step)
        return pltpu.make_async_remote_copy(
            src_ref=gram.at[pl.ds(pl.multiple_of(other * PIECE, PIECE), PIECE)], dst_ref=gparts.at[chip],
            send_sem=gr_send.at[slot(step)], recv_sem=gr_recv.at[chip], device_id=(peer(step), col), device_id_type=MESH,
        )

    def gram_arrived(step):
        other = away(step)
        return pltpu.make_async_remote_copy(
            src_ref=gram.at[pl.ds(0, PIECE)], dst_ref=gparts.at[other],
            send_sem=gr_send.at[slot(step)], recv_sem=gr_recv.at[other], device_id=(peer(step), col), device_id_type=MESH,
        )

    @pl.when(col == 0)
    def _():

        def one(block, carry):
            widen(block * BLOCK, BLOCK)
            return carry

        lax.fori_loop(0, BLOCKS, one, 0)
        full = cross(panel2[...], panel2[...])
        small = cross(panel2[:, :PANEL], panel3[...])
        small = small + small.T + full[PANEL:, PANEL:]
        gram[...] = full[:PANEL, :PANEL] + (full[:PANEL, PANEL:] + full[PANEL:, :PANEL] + small)

        await_round(0)
        announce(1)
        await_round(1)
        announce(2)
        await_round(2)
        for at in FAR:
            gram_piece(at).start()
        gparts[chip] = gram[pl.ds(pl.multiple_of(chip * PIECE, PIECE), PIECE)]

    wacc[...] = jnp.zeros_like(wacc)

    @pl.when(col == 0)
    def _():
        lax.fori_loop(0, BLOCKS, prepare, 0)

        def one(block, carry):
            accumulate(block * BLOCK, BLOCK)
            return carry

        lax.fori_loop(0, BLOCKS, one, 0)

    @pl.when(col != 0)
    def _():
        def ordered(step, right, head, count):
            turn = jnp.maximum(step - head, 0)
            both_ways = jnp.where(step < head, step, jnp.where(turn % 2 == 0, head, right) + turn // 2)
            straight = (step + jnp.where(col == 3, right, 0)) % count
            return jnp.where(col == 2, both_ways, straight)

        def pass_on(step):
            chunk = ordered(step, RIGHT, HEAD, CHUNKS)
            onward = jnp.where(chunk < RIGHT, col + 1, col - 1)
            shared = jnp.where(chunk < RIGHT, RIGHT - RIGHT_DIRECT, CHUNKS - LEFT_DIRECT)
            limit = jnp.where(col == 2, shared, CHUNKS)
            relay(chunk, 0).wait_recv()

            @pl.when((onward > 0) & (onward < 4) & (chunk < limit))
            def _():
                relay(chunk, onward).start()

        def work(index):
            unit = ordered(index, RIGHT // 2, HEAD // 2, UNITS)
            widen(unit * UNIT, UNIT)
            accumulate(unit * UNIT, UNIT)

        def pair_of_chunks(pair, carry):
            pass_on(2 * pair)
            work(pair - 1)
            pass_on(2 * pair + 1)

            @pl.when(pair == 1)
            def _():
                await_round(0)
                announce(1)

            @pl.when(pair == 2)
            def _():
                await_round(1)
                announce(2)

            @pl.when(pair == 4)
            def _():
                await_round(2)

            return carry

        announce(0)
        lax.fori_loop(0, BLOCKS - 2, prepare, 0)

        def rest(step, carry):
            @pl.when(col == 2)
            def _():
                prepare(BLOCKS - 2 + step, 0)

            pass_on(step)

            @pl.when(col != 2)
            def _():
                prepare(BLOCKS - 2 + step, 0)

            return carry

        lax.fori_loop(0, 2, rest, 0)
        lax.fori_loop(1, UNITS, pair_of_chunks, 0)
        work(UNITS - 1)

    exchange = pltpu.make_async_remote_copy(
        src_ref=wacc.at[:, pl.ds(pl.multiple_of((1 - core) * HALF, HALF), HALF)], dst_ref=swap,
        send_sem=ex_send, recv_sem=ex_recv, device_id=partner, device_id_type=MESH,
    )
    exchange.start()

    gram_swap = pltpu.make_async_remote_copy(
        src_ref=gsum, dst_ref=gswap, send_sem=gx_send, recv_sem=gx_recv, device_id=partner, device_id_type=MESH,
    )

    def gram_gather(step):
        rows = pl.ds(pl.multiple_of(chip * PIECE, PIECE), PIECE)
        return pltpu.make_async_remote_copy(
            src_ref=gfull.at[rows], dst_ref=gfull.at[rows],
            send_sem=ga_send.at[slot(step)], recv_sem=ga_recv.at[chip], device_id=(peer(step), col), device_id_type=MESH,
        )

    def gram_gathered(step):
        other = away(step)
        rows = pl.ds(pl.multiple_of(other * PIECE, PIECE), PIECE)
        return pltpu.make_async_remote_copy(
            src_ref=gfull.at[rows], dst_ref=gfull.at[rows],
            send_sem=ga_send.at[slot(step)], recv_sem=ga_recv.at[other], device_id=(peer(step), col), device_id_type=MESH,
        )

    @pl.when(col == 0)
    def _():
        for at in NEAR:
            gram_arrived(at).wait_recv()
        gsum[...] = jnp.sum(gparts[...], axis=0)
        gram_swap.start()
        gram_swap.wait()
        gfull[pl.ds(pl.multiple_of(chip * PIECE, PIECE), PIECE)] = gsum[...] + gswap[...]

        for at in FAR:
            gram_gather(at).start()

    exchange.wait()
    mine[...] = wacc[:, pl.ds(pl.multiple_of(core * HALF, HALF), HALF)] + swap[...]

    def scatter(step):
        other = away(step)
        return pltpu.make_async_remote_copy(
            src_ref=mine.at[pl.ds(pl.multiple_of(other * PIECE, PIECE), PIECE)], dst_ref=parts.at[chip],
            send_sem=rs_send.at[slot(step)], recv_sem=rs_recv.at[chip], device_id=(peer(step), col), device_id_type=MESH,
        )

    def scattered(step):
        other = away(step)
        return pltpu.make_async_remote_copy(
            src_ref=mine.at[pl.ds(0, PIECE)], dst_ref=parts.at[other],
            send_sem=rs_send.at[slot(step)], recv_sem=rs_recv.at[other], device_id=(peer(step), col), device_id_type=MESH,
        )

    for at in FAR:
        scatter(at).start()
    parts[chip] = mine[pl.ds(pl.multiple_of(chip * PIECE, PIECE), PIECE)]

    def sent_on(chunk, carry):
        relay(chunk, 0).wait_send()
        return carry

    @pl.when(col == 1)
    def _():
        lax.fori_loop(0, RIGHT, sent_on, 0)

    @pl.when(col == 2)
    def _():
        lax.fori_loop(0, RIGHT - RIGHT_DIRECT, sent_on, 0)
        lax.fori_loop(RIGHT, CHUNKS - LEFT_DIRECT, sent_on, 0)

    @pl.when(col == 3)
    def _():
        lax.fori_loop(RIGHT, CHUNKS, sent_on, 0)

    def send_packed(target):
        return pltpu.make_async_remote_copy(
            src_ref=packed, dst_ref=packed, send_sem=u_send.at[target], recv_sem=u_recv,
            device_id=(row, target), device_id_type=MESH,
        )

    @pl.when(col == 0)
    def _():
        for at in NEAR:
            gram_gathered(at).wait_recv()
        cholesky(gfull, packed)
        for target in (2, 1, 3):
            send_packed(target).start()

        def sent(chunk, carry):
            first(chunk, 1).wait_send()
            return carry

        lax.fori_loop(0, CHUNKS, sent, 0)

        for step in range(LEFT_DIRECT):
            first(CHUNKS - LEFT_DIRECT + step, 1, CHUNKS).wait_send()
        for step in range(RIGHT_DIRECT):
            first(RIGHT - RIGHT_DIRECT + step, 3, CHUNKS).wait_send()

    for at in NEAR:
        scattered(at).wait_recv()
    half = pl.ds(pl.multiple_of(core * HALF, HALF), HALF)
    own = pl.ds(pl.multiple_of(chip * PIECE, PIECE), PIECE)
    total[own, half] = jnp.sum(parts[...], axis=0)

    def gather(step):
        return pltpu.make_async_remote_copy(
            src_ref=total.at[own, half], dst_ref=total.at[own, half],
            send_sem=ag_send.at[slot(step)], recv_sem=ag_recv.at[chip], device_id=(peer(step), col), device_id_type=MESH,
        )

    def gathered(step):
        other = away(step)
        rows = pl.ds(pl.multiple_of(other * PIECE, PIECE), PIECE)
        return pltpu.make_async_remote_copy(
            src_ref=total.at[rows, half], dst_ref=total.at[rows, half],
            send_sem=ag_send.at[slot(step)], recv_sem=ag_recv.at[other], device_id=(peer(step), col), device_id_type=MESH,
        )

    def onward(owner, columns):
        rows = pl.ds(pl.multiple_of(owner * PIECE, PIECE), PIECE)
        return pltpu.make_async_remote_copy(
            src_ref=total.at[rows, columns], dst_ref=total.at[rows, columns], send_sem=fx_send.at[owner],
            recv_sem=fx_recv.at[owner], device_id=partner, device_id_type=MESH,
        )

    for at in FAR:
        gather(at).start()
    onward(chip, half).start()
    for at in NEAR:
        scatter(at).wait_send()
    for at in NEAR:
        gathered(at).wait_recv()
        onward(away(at), half).start()
    other_half = pl.ds(pl.multiple_of((1 - core) * HALF, HALF), HALF)

    for at in NEAR:
        gather(at).wait_send()

    @pl.when(col == 0)
    def _():
        for at in NEAR:
            gram_piece(at).wait_send()
            gram_gather(at).wait_send()
        for target in (2, 1, 3):
            send_packed(target).wait_send()

    @pl.when(col != 0)
    def _():
        send_packed(0).wait_recv()

    def finish(owner, carry):
        onward(owner, half).wait_send()
        onward(owner, other_half).wait_recv()
        return carry

    lax.fori_loop(0, CHIPS, finish, 0)


def apply_kernel(kept, panel2, total, packed, factor, coupling, updated, out, x2, sems):
    both = packed[...]
    sub = lax.broadcasted_iota(jnp.int32, (PANEL, PANEL), 0)
    lane = lax.broadcasted_iota(jnp.int32, (PANEL, PANEL), 1)
    factor[...] = jnp.where(lane >= sub, both, 0.0) * (1.0 / 256.0)
    lower = jnp.where(lane < sub, both, jnp.where(lane == sub, 1.0 / both, 0.0))
    to_coupling, to_weights = six_left(lower), six_left(lower.T)
    copies = []
    for n in range(COLS // TILE):
        columns = pl.ds(n * TILE, TILE)
        c = plain(to_coupling, six_right(total[:, columns]))
        coupling[:, columns] = c
        xh, xl = split(plain(to_weights, six_right(c)))
        x2[:, columns] = jnp.concatenate([xh, xh, xl], axis=0)
        for block in range(BLOCKS):
            rows = pl.ds(block * BLOCK, BLOCK)
            p = panel2[rows]
            left = jnp.concatenate([p, p[:, :PANEL]], axis=1)
            out[rows, columns] = kept[rows, columns] - plain(left, x2[:, columns])
            copy = pltpu.make_async_copy(
                out.at[rows, columns], updated.at[rows, columns], sems.at[n * BLOCKS + block]
            )
            copy.start()
            copies.append(copy)
    for copy in copies:
        copy.wait()


def body(snapshots):
    dma = pltpu.SemaphoreType.DMA
    snapshots = pltpu.with_memory_space_constraint(snapshots, pltpu.HBM)
    kept, panel2, total, packed = pl.pallas_call(
        gather_kernel,
        name="panel_sums",
        out_shape=[
            pltpu.VMEM((ROWS, COLS), F32),
            pltpu.VMEM((ROWS, 2 * PANEL), BF16),
            pltpu.VMEM((PANEL, COLS), F32),
            pltpu.VMEM((PANEL, PANEL), F32),
        ],
        in_specs=[pl.BlockSpec(memory_space=pltpu.HBM)],
        out_specs=[pl.BlockSpec(memory_space=pltpu.VMEM)] * 4,
        scratch_shapes=[
            pltpu.VMEM((ROWS, PANEL), F32),
            pltpu.VMEM((ROWS, COLS), BF16),
            pltpu.VMEM((ROWS, COLS), BF16),
            pltpu.VMEM((ROWS, COLS), BF16),
            pltpu.VMEM((ROWS, PANEL), BF16),
            pltpu.VMEM((PANEL, COLS), F32),
            pltpu.VMEM((PANEL, HALF), F32),
            pltpu.VMEM((PANEL, HALF), F32),
            pltpu.VMEM((CHIPS, PIECE, HALF), F32),
            pltpu.VMEM((PANEL, PANEL), F32),
            pltpu.VMEM((CHIPS, PIECE, PANEL), F32),
            pltpu.VMEM((PIECE, PANEL), F32),
            pltpu.VMEM((PIECE, PANEL), F32),
            pltpu.VMEM((PANEL, PANEL), F32),
            dma((BLOCKS,)), dma, dma((2 * CHUNKS,)), dma((CHUNKS,)), dma, dma,
            dma((CHIPS,)), dma((CHIPS,)), dma((CHIPS,)), dma((CHIPS,)), dma((CHIPS,)), dma((CHIPS,)),
            dma((CHIPS,)), dma((CHIPS,)), dma, dma, dma((CHIPS,)), dma((CHIPS,)), dma((4,)), dma,
            pltpu.SemaphoreType.REGULAR((3,)),
        ],
        compiler_params=pltpu.CompilerParams(
            collective_id=0, has_side_effects=True, vmem_limit_bytes=30 << 20
        ),
    )(snapshots)
    kept, panel2, total, packed = [
        pltpu.with_memory_space_constraint(a, pltpu.VMEM) for a in (kept, panel2, total, packed)
    ]
    return pl.pallas_call(
        apply_kernel,
        name="apply",
        out_shape=[
            jax.ShapeDtypeStruct((PANEL, PANEL), F32),
            jax.ShapeDtypeStruct((PANEL, COLS), F32),
            jax.ShapeDtypeStruct((ROWS, COLS), F32),
        ],
        in_specs=[pl.BlockSpec(memory_space=pltpu.VMEM)] * 4,
        out_specs=[
            pl.BlockSpec(memory_space=pltpu.VMEM),
            pl.BlockSpec(memory_space=pltpu.VMEM),
            pl.BlockSpec(memory_space=pl.ANY),
        ],
        scratch_shapes=[
            pltpu.VMEM((ROWS, COLS), F32),
            pltpu.VMEM((3 * PANEL, COLS), BF16),
            dma((BLOCKS * COLS // TILE,)),
        ],
        compiler_params=pltpu.CompilerParams(vmem_limit_bytes=24 << 20),
    )(kept, panel2, total, packed)


def solution(mesh):
    in_specs = (P("rows", "cols"),)
    out_specs = (P(), P(None, "cols"), P("rows", "cols"))
    return jax.shard_map(body, mesh=mesh, in_specs=in_specs, out_specs=out_specs, check_vma=False)
```

```python
import jax
import jax.numpy as jnp
from jax import lax
from jax.experimental import pallas as pl
from jax.experimental.pallas import tpu as pltpu
from jax.sharding import PartitionSpec as P

MESH = pl.DeviceIdType.MESH
F32 = jnp.float32
BF16 = jnp.bfloat16
PANEL = 128
ROWS = 2048
COLS = 1024
HALF = COLS // 2
CHIPS = 16
BLOCK = 256
BLOCKS = ROWS // BLOCK
CHUNK = 64
CHUNKS = ROWS // CHUNK
RIGHT = 16
LEFT = CHUNKS - RIGHT
HEAD = RIGHT - LEFT
RIGHT_DIRECT = 6
LEFT_DIRECT = 8
PER = BLOCK // CHUNK
PIECE = PANEL // CHIPS
TILE = 512
GROUP = 16
SIZE = 4
UNIT = 128
UNITS = ROWS // UNIT
NEAR = sorted(
    ((dz, dy) for dz in range(SIZE) for dy in range(SIZE) if dz or dy),
    key=lambda at: min(at[0], SIZE - at[0]) + min(at[1], SIZE - at[1]),
)
FAR = NEAR[::-1]


def slot(at):
    return at[0] * SIZE + at[1]


def split(value):
    high = value.astype(BF16)
    low = (value - high.astype(F32)).astype(BF16)
    return high, low


def cross(left, right):
    return lax.dot_general(left, right, (((0,), (0,)), ((), ())), preferred_element_type=F32)


def plain(left, right):
    return lax.dot_general(left, right, (((1,), (0,)), ((), ())), preferred_element_type=F32)


def inverse(value):
    guess = pl.reciprocal(value, approx=True)
    return guess * (2.0 - value * guess)


def triple(value):
    one = value.astype(BF16)
    rest = value - one.astype(F32)
    two = rest.astype(BF16)
    return one, two, (rest - two.astype(F32)).astype(BF16)


def six_left(value):
    one, two, three = triple(value)
    return jnp.concatenate([one, one, two, two, one, three], axis=1)


def six_right(value):
    one, two, three = triple(value)
    return jnp.concatenate([one, two, one, two, three, one], axis=0)


def cholesky(gram_ref, packed_ref):
    shape = (GROUP, PANEL)
    sub = lax.broadcasted_iota(jnp.int32, shape, 0)
    lane = lax.broadcasted_iota(jnp.int32, shape, 1)

    def across(value, k):
        return jnp.broadcast_to(value[k : k + 1, :], shape)

    count = PANEL // GROUP
    lefts = [gram_ref[n * GROUP : (n + 1) * GROUP, :] for n in range(count)]
    rights = [(lane == sub + n * GROUP).astype(F32) for n in range(count)]
    for n in range(count):
        base = n * GROUP
        top, side = lefts[n], rights[n]
        columns = [jnp.broadcast_to(top[:, base + k : base + k + 1], shape) for k in range(GROUP)]
        pivot = across(columns[0], 0)
        pivots = pivot
        for k in range(GROUP - 1):
            recip = inverse(pivot)
            link = across(columns[k + 1], k)
            pivot = across(columns[k + 1], k + 1) - (link * recip) * link
            pivots = jnp.where(sub > k, pivot, pivots)
            factor = jnp.where(sub > k, columns[k] * recip, 0.0)
            for j in range(k + 1, GROUP):
                columns[j] = columns[j] - factor * across(columns[j], k)
            top, side = top - factor * across(top, k), side - factor * across(side, k)
        scale = lax.rsqrt(pivots)
        scale = scale * (1.5 - 0.5 * pivots * scale * scale)
        top = jnp.where(lane >= sub + base, top * scale, 0.0)
        side = side * scale
        packed_ref[base : base + GROUP, :] = jnp.where(lane >= sub + base, top, side)
        if n + 1 < count:
            one, two, three = triple(jnp.concatenate([top, side], axis=1))
            update = cross(
                jnp.concatenate([v[:, :PANEL] for v in (one, one, two, two, one, three)], axis=0),
                jnp.concatenate([one, two, one, two, three, one], axis=0),
            )
            for m in range(n + 1, count):
                rows = update[m * GROUP : (m + 1) * GROUP]
                lefts[m] = lefts[m] - rows[:, :PANEL]
                rights[m] = rights[m] - rows[:, PANEL:]


def gather_kernel(
    snap, kept, panel2, total, packed,
    pbuf, high, low, third, panel3, wacc, swap, mine, parts, gram, gparts, gsum, gswap, gfull,
    load_sem, pload_sem, bs_send, bs_recv, ex_send, ex_recv, rs_send, rs_recv, ag_send, ag_recv,
    fx_send, fx_recv, gr_send, gr_recv, gx_send, gx_recv, ga_send, ga_recv, u_send, u_recv, meet,
):
    row = lax.axis_index("rows")
    col = lax.axis_index("cols")
    chip = row // 2
    core = row % 2
    partner = (chip * 2 + 1 - core, col)
    high_axis, low_axis = chip // SIZE, chip % SIZE

    def away(at):
        return ((high_axis + at[0]) % SIZE) * SIZE + (low_axis + at[1]) % SIZE

    def peer(at):
        return away(at) * 2 + core

    along_x = [(row, (col + step) % SIZE) for step in (1, SIZE - 1)]
    along_low = [(peer((0, step)), col) for step in (1, SIZE - 1)]
    along_high = [(peer((step, 0)), col) for step in (1, SIZE - 1)]
    rounds = [along_x + along_low, along_high, along_high]

    def announce(index):
        for other in rounds[index]:
            pl.semaphore_signal(meet.at[index], inc=1, device_id=other, device_id_type=MESH)

    def await_round(index):
        pl.semaphore_wait(meet.at[index], len(rounds[index]))

    greeted = along_x + along_low + along_high + [partner]
    barrier = pltpu.get_barrier_semaphore()
    for other in greeted:
        pl.semaphore_signal(barrier, inc=1, device_id=other, device_id_type=MESH)

    def load(block):
        rows = pl.ds(pl.multiple_of(block * BLOCK, BLOCK), BLOCK)
        return pltpu.make_async_copy(snap.at[rows], kept.at[rows], load_sem.at[block])

    panel_load = pltpu.make_async_copy(snap.at[:, pl.ds(0, PANEL)], pbuf, pload_sem)

    @pl.when(col == 0)
    def _():
        panel_load.start()

    def start_load(block, carry):
        load(block).start()
        return carry

    @pl.when(col != 0)
    def _():
        lax.fori_loop(0, BLOCKS, start_load, 0)

    pl.semaphore_wait(barrier, len(greeted))

    def chunk_rows(chunk):
        return pl.ds(pl.multiple_of(chunk * CHUNK, CHUNK), CHUNK)

    def relay(chunk, target):
        rows = chunk_rows(chunk)
        return pltpu.make_async_remote_copy(
            src_ref=pbuf.at[rows], dst_ref=pbuf.at[rows], send_sem=bs_send.at[chunk],
            recv_sem=bs_recv.at[chunk], device_id=(row, target), device_id_type=MESH,
        )

    def first(chunk, target, extra=0):
        rows = chunk_rows(chunk)
        return pltpu.make_async_remote_copy(
            src_ref=pbuf.at[rows], dst_ref=pbuf.at[rows], send_sem=bs_send.at[chunk + extra],
            recv_sem=bs_recv.at[chunk], device_id=(row, target), device_id_type=MESH,
        )

    @pl.when(col == 0)
    def _():
        def send_right(step, carry):
            first(step, 1).start()
            return carry

        def send(step, carry):
            first(step + HEAD, 1).start()
            first(step + RIGHT, 3).start()
            return carry

        panel_load.wait()
        lax.fori_loop(0, HEAD, send_right, 0)
        lax.fori_loop(0, LEFT, send, 0)
        for step in range(max(RIGHT_DIRECT, LEFT_DIRECT)):
            if step < LEFT_DIRECT:
                first(CHUNKS - LEFT_DIRECT + step, 1, CHUNKS).start()
            if step < RIGHT_DIRECT:
                first(RIGHT - RIGHT_DIRECT + step, 3, CHUNKS).start()
        lax.fori_loop(0, BLOCKS, start_load, 0)
        announce(0)

    def block_rows(block):
        return pl.ds(pl.multiple_of(block * BLOCK, BLOCK), BLOCK)

    def widen(start, size):
        rows = pl.ds(pl.multiple_of(start, size), size)
        one, two, three = triple(pbuf[rows])
        panel2[rows, :PANEL] = one
        panel2[rows, PANEL:] = two
        panel3[rows] = three

    def prepare(block, carry):
        load(block).wait()
        rows = block_rows(block)
        high[rows], low[rows], third[rows] = triple(kept[rows])
        return carry

    def accumulate(start, size, tiles=range(COLS // 256)):
        rows = pl.ds(pl.multiple_of(start, size), size)
        turned = jnp.concatenate([panel2[rows], panel3[rows]], axis=1).T
        for n in tiles:
            columns = pl.ds(n * 256, 256)
            one = plain(turned, high[rows, columns])
            two = plain(turned[: 2 * PANEL], low[rows, columns])
            three = plain(turned[:PANEL], third[rows, columns])
            small = one[2 * PANEL :] + two[PANEL:] + three
            wacc[:, columns] += one[:PANEL] + (one[PANEL : 2 * PANEL] + two[:PANEL] + small)

    def gram_piece(step):
        other = away(step)
        return pltpu.make_async_remote_copy(
            src_ref=gram.at[pl.ds(pl.multiple_of(other * PIECE, PIECE), PIECE)], dst_ref=gparts.at[chip],
            send_sem=gr_send.at[slot(step)], recv_sem=gr_recv.at[chip], device_id=(peer(step), col), device_id_type=MESH,
        )

    def gram_arrived(step):
        other = away(step)
        return pltpu.make_async_remote_copy(
            src_ref=gram.at[pl.ds(0, PIECE)], dst_ref=gparts.at[other],
            send_sem=gr_send.at[slot(step)], recv_sem=gr_recv.at[other], device_id=(peer(step), col), device_id_type=MESH,
        )

    @pl.when(col == 0)
    def _():

        def one(block, carry):
            widen(block * BLOCK, BLOCK)
            return carry

        lax.fori_loop(0, BLOCKS, one, 0)
        full = cross(panel2[...], panel2[...])
        small = cross(panel2[:, :PANEL], panel3[...])
        small = small + small.T + full[PANEL:, PANEL:]
        gram[...] = full[:PANEL, :PANEL] + (full[:PANEL, PANEL:] + full[PANEL:, :PANEL] + small)

        await_round(0)
        announce(1)
        await_round(1)
        announce(2)
        await_round(2)
        for at in FAR:
            gram_piece(at).start()
        gparts[chip] = gram[pl.ds(pl.multiple_of(chip * PIECE, PIECE), PIECE)]

    exchange = pltpu.make_async_remote_copy(
        src_ref=wacc.at[:, pl.ds(pl.multiple_of((1 - core) * HALF, HALF), HALF)], dst_ref=swap,
        send_sem=ex_send, recv_sem=ex_recv, device_id=partner, device_id_type=MESH,
    )
    wacc[...] = jnp.zeros_like(wacc)

    @pl.when(col == 0)
    def _():
        lax.fori_loop(0, BLOCKS, prepare, 0)

        def one(block, carry):
            accumulate(block * BLOCK, BLOCK)
            return carry

        lax.fori_loop(0, BLOCKS, one, 0)
        exchange.start()

    @pl.when(col != 0)
    def _():
        def ordered(step, right, head, count):
            turn = jnp.maximum(step - head, 0)
            both_ways = jnp.where(step < head, step, jnp.where(turn % 2 == 0, head, right) + turn // 2)
            straight = (step + jnp.where(col == 3, right, 0)) % count
            return jnp.where(col == 2, both_ways, straight)

        def pass_on(step):
            chunk = ordered(step, RIGHT, HEAD, CHUNKS)
            onward = jnp.where(chunk < RIGHT, col + 1, col - 1)
            shared = jnp.where(chunk < RIGHT, RIGHT - RIGHT_DIRECT, CHUNKS - LEFT_DIRECT)
            limit = jnp.where(col == 2, shared, CHUNKS)
            relay(chunk, 0).wait_recv()

            @pl.when((onward > 0) & (onward < 4) & (chunk < limit))
            def _():
                relay(chunk, onward).start()

        def work(index):
            unit = ordered(index, RIGHT // 2, HEAD // 2, UNITS)
            widen(unit * UNIT, UNIT)
            accumulate(unit * UNIT, UNIT)

        def pair_of_chunks(pair, carry):
            pass_on(2 * pair)
            work(pair - 1)
            pass_on(2 * pair + 1)

            @pl.when(pair == 1)
            def _():
                await_round(0)
                announce(1)

            @pl.when(pair == 2)
            def _():
                await_round(1)
                announce(2)

            @pl.when(pair == 4)
            def _():
                await_round(2)

            return carry

        announce(0)
        lax.fori_loop(0, BLOCKS - 2, prepare, 0)

        def rest(step, carry):
            @pl.when(col == 2)
            def _():
                prepare(BLOCKS - 2 + step, 0)

            pass_on(step)

            @pl.when(col != 2)
            def _():
                prepare(BLOCKS - 2 + step, 0)

            return carry

        lax.fori_loop(0, 2, rest, 0)
        lax.fori_loop(1, UNITS, pair_of_chunks, 0)
        last = ordered(UNITS - 1, RIGHT // 2, HEAD // 2, UNITS) * UNIT
        widen(last, UNIT)

        @pl.when(core == 0)
        def _():
            accumulate(last, UNIT, (2, 3))
            exchange.start()
            accumulate(last, UNIT, (0, 1))

        @pl.when(core != 0)
        def _():
            accumulate(last, UNIT, (0, 1))
            exchange.start()
            accumulate(last, UNIT, (2, 3))

    gram_swap = pltpu.make_async_remote_copy(
        src_ref=gsum, dst_ref=gswap, send_sem=gx_send, recv_sem=gx_recv, device_id=partner, device_id_type=MESH,
    )

    def gram_gather(step):
        rows = pl.ds(pl.multiple_of(chip * PIECE, PIECE), PIECE)
        return pltpu.make_async_remote_copy(
            src_ref=gfull.at[rows], dst_ref=gfull.at[rows],
            send_sem=ga_send.at[slot(step)], recv_sem=ga_recv.at[chip], device_id=(peer(step), col), device_id_type=MESH,
        )

    def gram_gathered(step):
        other = away(step)
        rows = pl.ds(pl.multiple_of(other * PIECE, PIECE), PIECE)
        return pltpu.make_async_remote_copy(
            src_ref=gfull.at[rows], dst_ref=gfull.at[rows],
            send_sem=ga_send.at[slot(step)], recv_sem=ga_recv.at[other], device_id=(peer(step), col), device_id_type=MESH,
        )

    @pl.when(col == 0)
    def _():
        for at in NEAR:
            gram_arrived(at).wait_recv()
        gsum[...] = jnp.sum(gparts[...], axis=0)
        gram_swap.start()
        gram_swap.wait()
        gfull[pl.ds(pl.multiple_of(chip * PIECE, PIECE), PIECE)] = gsum[...] + gswap[...]

        for at in FAR:
            gram_gather(at).start()

    exchange.wait()
    mine[...] = wacc[:, pl.ds(pl.multiple_of(core * HALF, HALF), HALF)] + swap[...]

    def scatter(step):
        other = away(step)
        return pltpu.make_async_remote_copy(
            src_ref=mine.at[pl.ds(pl.multiple_of(other * PIECE, PIECE), PIECE)], dst_ref=parts.at[chip],
            send_sem=rs_send.at[slot(step)], recv_sem=rs_recv.at[chip], device_id=(peer(step), col), device_id_type=MESH,
        )

    def scattered(step):
        other = away(step)
        return pltpu.make_async_remote_copy(
            src_ref=mine.at[pl.ds(0, PIECE)], dst_ref=parts.at[other],
            send_sem=rs_send.at[slot(step)], recv_sem=rs_recv.at[other], device_id=(peer(step), col), device_id_type=MESH,
        )

    for at in FAR:
        scatter(at).start()
    parts[chip] = mine[pl.ds(pl.multiple_of(chip * PIECE, PIECE), PIECE)]

    def sent_on(chunk, carry):
        relay(chunk, 0).wait_send()
        return carry

    @pl.when(col == 1)
    def _():
        lax.fori_loop(0, RIGHT, sent_on, 0)

    @pl.when(col == 2)
    def _():
        lax.fori_loop(0, RIGHT - RIGHT_DIRECT, sent_on, 0)
        lax.fori_loop(RIGHT, CHUNKS - LEFT_DIRECT, sent_on, 0)

    @pl.when(col == 3)
    def _():
        lax.fori_loop(RIGHT, CHUNKS, sent_on, 0)

    def send_packed(target):
        return pltpu.make_async_remote_copy(
            src_ref=packed, dst_ref=packed, send_sem=u_send.at[target], recv_sem=u_recv,
            device_id=(row, target), device_id_type=MESH,
        )

    @pl.when(col == 0)
    def _():
        for at in NEAR:
            gram_gathered(at).wait_recv()
        cholesky(gfull, packed)
        for target in (2, 1, 3):
            send_packed(target).start()

        def sent(chunk, carry):
            first(chunk, 1).wait_send()
            return carry

        lax.fori_loop(0, CHUNKS, sent, 0)

        for step in range(LEFT_DIRECT):
            first(CHUNKS - LEFT_DIRECT + step, 1, CHUNKS).wait_send()
        for step in range(RIGHT_DIRECT):
            first(RIGHT - RIGHT_DIRECT + step, 3, CHUNKS).wait_send()

    for at in NEAR:
        scattered(at).wait_recv()
    half = pl.ds(pl.multiple_of(core * HALF, HALF), HALF)
    own = pl.ds(pl.multiple_of(chip * PIECE, PIECE), PIECE)
    total[own, half] = jnp.sum(parts[...], axis=0)

    def gather(step):
        return pltpu.make_async_remote_copy(
            src_ref=total.at[own, half], dst_ref=total.at[own, half],
            send_sem=ag_send.at[slot(step)], recv_sem=ag_recv.at[chip], device_id=(peer(step), col), device_id_type=MESH,
        )

    def gathered(step):
        other = away(step)
        rows = pl.ds(pl.multiple_of(other * PIECE, PIECE), PIECE)
        return pltpu.make_async_remote_copy(
            src_ref=total.at[rows, half], dst_ref=total.at[rows, half],
            send_sem=ag_send.at[slot(step)], recv_sem=ag_recv.at[other], device_id=(peer(step), col), device_id_type=MESH,
        )

    def onward(owner, columns):
        rows = pl.ds(pl.multiple_of(owner * PIECE, PIECE), PIECE)
        return pltpu.make_async_remote_copy(
            src_ref=total.at[rows, columns], dst_ref=total.at[rows, columns], send_sem=fx_send.at[owner],
            recv_sem=fx_recv.at[owner], device_id=partner, device_id_type=MESH,
        )

    for at in FAR:
        gather(at).start()
    onward(chip, half).start()
    for at in NEAR:
        scatter(at).wait_send()
    for at in NEAR:
        gathered(at).wait_recv()
        onward(away(at), half).start()
    other_half = pl.ds(pl.multiple_of((1 - core) * HALF, HALF), HALF)

    for at in NEAR:
        gather(at).wait_send()

    @pl.when(col == 0)
    def _():
        for at in NEAR:
            gram_piece(at).wait_send()
            gram_gather(at).wait_send()
        for target in (2, 1, 3):
            send_packed(target).wait_send()

    @pl.when(col != 0)
    def _():
        send_packed(0).wait_recv()

    def finish(owner, carry):
        onward(owner, half).wait_send()
        onward(owner, other_half).wait_recv()
        return carry

    lax.fori_loop(0, CHIPS, finish, 0)


def apply_kernel(kept, panel2, total, packed, factor, coupling, updated, out, x2, sems):
    both = packed[...]
    sub = lax.broadcasted_iota(jnp.int32, (PANEL, PANEL), 0)
    lane = lax.broadcasted_iota(jnp.int32, (PANEL, PANEL), 1)
    factor[...] = jnp.where(lane >= sub, both, 0.0) * (1.0 / 256.0)
    lower = jnp.where(lane < sub, both, jnp.where(lane == sub, 1.0 / both, 0.0))
    to_coupling, to_weights = six_left(lower), six_left(lower.T)
    copies = []
    for n in range(COLS // TILE):
        columns = pl.ds(n * TILE, TILE)
        c = plain(to_coupling, six_right(total[:, columns]))
        coupling[:, columns] = c
        xh, xl = split(plain(to_weights, six_right(c)))
        x2[:, columns] = jnp.concatenate([xh, xh, xl], axis=0)
        for block in range(BLOCKS):
            rows = pl.ds(block * BLOCK, BLOCK)
            p = panel2[rows]
            left = jnp.concatenate([p, p[:, :PANEL]], axis=1)
            out[rows, columns] = kept[rows, columns] - plain(left, x2[:, columns])
            copy = pltpu.make_async_copy(
                out.at[rows, columns], updated.at[rows, columns], sems.at[n * BLOCKS + block]
            )
            copy.start()
            copies.append(copy)
    for copy in copies:
        copy.wait()


def body(snapshots):
    dma = pltpu.SemaphoreType.DMA
    snapshots = pltpu.with_memory_space_constraint(snapshots, pltpu.HBM)
    kept, panel2, total, packed = pl.pallas_call(
        gather_kernel,
        name="panel_sums",
        out_shape=[
            pltpu.VMEM((ROWS, COLS), F32),
            pltpu.VMEM((ROWS, 2 * PANEL), BF16),
            pltpu.VMEM((PANEL, COLS), F32),
            pltpu.VMEM((PANEL, PANEL), F32),
        ],
        in_specs=[pl.BlockSpec(memory_space=pltpu.HBM)],
        out_specs=[pl.BlockSpec(memory_space=pltpu.VMEM)] * 4,
        scratch_shapes=[
            pltpu.VMEM((ROWS, PANEL), F32),
            pltpu.VMEM((ROWS, COLS), BF16),
            pltpu.VMEM((ROWS, COLS), BF16),
            pltpu.VMEM((ROWS, COLS), BF16),
            pltpu.VMEM((ROWS, PANEL), BF16),
            pltpu.VMEM((PANEL, COLS), F32),
            pltpu.VMEM((PANEL, HALF), F32),
            pltpu.VMEM((PANEL, HALF), F32),
            pltpu.VMEM((CHIPS, PIECE, HALF), F32),
            pltpu.VMEM((PANEL, PANEL), F32),
            pltpu.VMEM((CHIPS, PIECE, PANEL), F32),
            pltpu.VMEM((PIECE, PANEL), F32),
            pltpu.VMEM((PIECE, PANEL), F32),
            pltpu.VMEM((PANEL, PANEL), F32),
            dma((BLOCKS,)), dma, dma((2 * CHUNKS,)), dma((CHUNKS,)), dma, dma,
            dma((CHIPS,)), dma((CHIPS,)), dma((CHIPS,)), dma((CHIPS,)), dma((CHIPS,)), dma((CHIPS,)),
            dma((CHIPS,)), dma((CHIPS,)), dma, dma, dma((CHIPS,)), dma((CHIPS,)), dma((4,)), dma,
            pltpu.SemaphoreType.REGULAR((3,)),
        ],
        compiler_params=pltpu.CompilerParams(
            collective_id=0, has_side_effects=True, vmem_limit_bytes=30 << 20
        ),
    )(snapshots)
    kept, panel2, total, packed = [
        pltpu.with_memory_space_constraint(a, pltpu.VMEM) for a in (kept, panel2, total, packed)
    ]
    return pl.pallas_call(
        apply_kernel,
        name="apply",
        out_shape=[
            jax.ShapeDtypeStruct((PANEL, PANEL), F32),
            jax.ShapeDtypeStruct((PANEL, COLS), F32),
            jax.ShapeDtypeStruct((ROWS, COLS), F32),
        ],
        in_specs=[pl.BlockSpec(memory_space=pltpu.VMEM)] * 4,
        out_specs=[
            pl.BlockSpec(memory_space=pltpu.VMEM),
            pl.BlockSpec(memory_space=pltpu.VMEM),
            pl.BlockSpec(memory_space=pl.ANY),
        ],
        scratch_shapes=[
            pltpu.VMEM((ROWS, COLS), F32),
            pltpu.VMEM((3 * PANEL, COLS), BF16),
            dma((BLOCKS * COLS // TILE,)),
        ],
        compiler_params=pltpu.CompilerParams(vmem_limit_bytes=24 << 20),
    )(kept, panel2, total, packed)


def solution(mesh):
    in_specs = (P("rows", "cols"),)
    out_specs = (P(), P(None, "cols"), P("rows", "cols"))
    return jax.shard_map(body, mesh=mesh, in_specs=in_specs, out_specs=out_specs, check_vma=False)
```
